256 devices in a mesh: batch: 2 (over core), queue: 128 (over x, y, z).
Axes of the slice: x: 4, y: 4, z: 8, core: 2. Of those that a mesh axis runs over, the one named last changes fastest.
Arguments:
- queries: bfloat16 [2048, 1024], P('batch'), may hold values from -128 to 128
- queue: bfloat16 [196608, 1024], P('queue'), may hold values from -8 to 8
- mentor_logit_grid: bfloat16 [2048, 196608], P('batch', 'queue'), may hold values from -40 to 260
- positives: int32 [2048], P('batch'), may hold values from 0 to 196607
Outputs:
- query_grad: float32 [2048, 1024], P('batch')
- loss: float32 [], replicated
The draws below stay inside these ranges and needn't reach their ends.
All inputs are finite; a program needn't handle non-finite values.
Results may differ from the reference program's by a relative error of at most 0.0026.
Values sent between devices are 32-bit elements; how exact they have to be, the bound alone decides.
No kernel may reach another device: no remote copies, remote signals or barrier semaphores. Data moves between devices by JAX's collectives and lax.ppermute only.
A program may use at most 64 MiB of HBM per device.

```python
import math
import jax
import jax.numpy as jnp
from jax import lax

D = 1024
KEYS_DEV = 1536
BATCH = 2048
KEYS = 196608
N_QUEUE = 128


def queue_seed(key):
    return jax.random.fold_in(key, 11)


def key_vector(seed_key, row_index):
    row_key = jax.random.fold_in(seed_key, row_index)
    ramp_factor = 1.0 + 0.2 * row_index.astype(jnp.float32) / KEYS
    entries = jnp.clip(jax.random.normal(row_key, (D,), jnp.float32), -4.0, 4.0)
    return entries * ramp_factor


def draw_queue(key, part):
    seed_key = queue_seed(key)

    def one_row(row_index):
        return key_vector(seed_key, row_index)
    vectors = jax.vmap(one_row)(jnp.arange(KEYS, dtype=jnp.int32))
    return vectors.astype(jnp.bfloat16)


def draw_queries(key, part):
    noise_key = jax.random.fold_in(key, 21)
    drawn_rows = jnp.clip(jax.random.normal(noise_key, (BATCH, D), jnp.float32), -6.0, 6.0)
    return drawn_rows.astype(jnp.bfloat16)


def draw_mentor_logit_grid(key, part):
    noise_key = jax.random.fold_in(key, 31)
    ramp_factor = 1.1 * jnp.arange(KEYS, dtype=jnp.float32) / KEYS
    values = 3.0 * jnp.clip(jax.random.normal(noise_key, (BATCH, KEYS), jnp.float32), -6.0, 6.0) + ramp_factor[None, :]
    return values.astype(jnp.bfloat16)


def place_ends(drawn, own_key, least, largest):
    index_at = [jax.random.randint(jax.random.fold_in(own_key, axis), (), 0, length) for axis, length in enumerate(drawn.shape)]
    main_axis = drawn.shape.index(max(drawn.shape))
    next_to = index_at[:main_axis] + [(index_at[main_axis] + 1) % drawn.shape[main_axis]] + index_at[main_axis + 1:]
    return drawn.at[tuple(index_at)].set(least).at[tuple(next_to)].set(largest)


def setup_inputs(seed: int = 0) -> dict:
    key_of = jax.random.split(jax.random.key(seed), 5)
    return {
        "queries": draw_queries(jax.random.fold_in(key_of[4], 71), 0),
        "queue": draw_queue(jax.random.fold_in(key_of[4], 71), 0),
        "mentor_logit_grid": draw_mentor_logit_grid(jax.random.fold_in(key_of[4], 71), 0),
        "positives": place_ends(jax.random.randint(key_of[3], (BATCH,), 0, KEYS), jax.random.fold_in(key_of[3], 1), 0, KEYS - 1).astype(jnp.int32),
    }


score_factor = 3.0
reward_value = 12.0
floor_value = -1e+30

def merge_stats(earlier, latter):
    stud_top = jnp.maximum(earlier[0], latter[0])
    stud_total = earlier[1] * jnp.exp(earlier[0] - stud_top) + latter[1] * jnp.exp(latter[0] - stud_top)
    teach_top = jnp.maximum(earlier[2], latter[2])
    early_factor = jnp.exp(earlier[2] - teach_top)
    late_factor = jnp.exp(latter[2] - teach_top)
    teach_total = earlier[3] * early_factor + latter[3] * late_factor
    cross_total = earlier[4] * early_factor + latter[4] * late_factor
    return (stud_top, stud_total, teach_top, teach_total, cross_total)

def local_stats(scores, mentor_model):
    stud_max = lax.optimization_barrier(jnp.max(scores, axis=1))
    stud_sum = lax.optimization_barrier(jnp.sum(jnp.exp(scores - stud_max[:, None]), axis=1))
    teach_max = lax.optimization_barrier(jnp.max(mentor_model, axis=1))
    teach_exp = jnp.exp(mentor_model - teach_max[:, None])
    teach_sum = lax.optimization_barrier(jnp.sum(teach_exp, axis=1))
    cross_sum = lax.optimization_barrier(jnp.sum(teach_exp * (mentor_model - scores), axis=1))
    return (stud_max, stud_sum, teach_max, teach_sum, cross_sum)

def block_terms(query_values, key_block, mentor_block, positives, offset, score_scale):
    scores = score_scale * jnp.einsum('rd,kd->rk', query_values, key_block.astype(jnp.float32))
    key_index = offset + jnp.arange(key_block.shape[0], dtype=jnp.int32)
    positive_match = (key_index[None, :] == positives[:, None]).astype(jnp.float32)
    mentor_model = mentor_block.astype(jnp.float32) + reward_value * positive_match
    return (scores, mentor_model)

def reference(queries, queue, mentor_logit_grid, positives):
    score_scale = score_factor / math.sqrt(D)
    query_values = queries.astype(jnp.float32)
    key_blocks = queue.reshape(N_QUEUE, KEYS_DEV, D)
    teach_blocks = jnp.transpose(mentor_logit_grid.reshape(BATCH, N_QUEUE, KEYS_DEV), (1, 0, 2))
    block_ids = jnp.arange(N_QUEUE, dtype=jnp.int32)

    def first_pass(running, inputs):
        key_block, mentor_block, block_id = inputs
        scores, mentor_model = block_terms(query_values, key_block, mentor_block, positives, block_id * KEYS_DEV, score_scale)
        return (merge_stats(running, local_stats(scores, mentor_model)), None)
    zeros_rows = jnp.zeros((BATCH,), jnp.float32)
    floor_rows = jnp.full((BATCH,), floor_value, jnp.float32)
    initial = (floor_rows, zeros_rows, floor_rows, zeros_rows, zeros_rows)
    merged_stats, _ = lax.scan(first_pass, initial, (key_blocks, teach_blocks, block_ids))
    stud_log = merged_stats[0] + jnp.log(merged_stats[1])
    teach_log = merged_stats[2] + jnp.log(merged_stats[3])
    divergence = merged_stats[4] / merged_stats[3] - teach_log + stud_log

    def second_pass(running, inputs):
        key_block, mentor_block, block_id = inputs
        scores, mentor_model = block_terms(query_values, key_block, mentor_block, positives, block_id * KEYS_DEV, score_scale)
        weights = (jnp.exp(scores - stud_log[:, None]) - jnp.exp(mentor_model - teach_log[:, None])).astype(jnp.bfloat16)
        weights = lax.optimization_barrier(weights)
        update = jnp.einsum('rk,kd->rd', weights.astype(jnp.float32), key_block.astype(jnp.float32))
        return (running + update, None)
    query_grad, _ = lax.scan(second_pass, jnp.zeros((BATCH, D), jnp.float32), (key_blocks, teach_blocks, block_ids))
    loss = jnp.sum(divergence) / BATCH
    return (query_grad, loss)
```

```python
import math

import jax
import jax.numpy as jnp
from jax import lax
from jax.sharding import Mesh
from jax.sharding import PartitionSpec as P

X, Y, Z = "queue_0", "queue_1", "queue_2"
QUEUE = (X, Y, Z)

score_factor = 3.0
reward_value = 12.0


def exchanged(part, axis, k):
    n = lax.axis_size(axis)
    return lax.ppermute(part, axis, [(i, i ^ k) for i in range(n)])


def scattered_sum(parts, axis):
    me = lax.axis_index(axis)
    total = lax.dynamic_index_in_dim(parts, me, 0, False)
    for k in (2, 1, 3):
        mine = lax.dynamic_index_in_dim(parts, me ^ k, 0, False)
        total = total + exchanged(mine, axis, k)
    return total


def gathered(part, axis):
    me = lax.axis_index(axis)
    out = jnp.zeros((lax.axis_size(axis), *part.shape), part.dtype)
    for k, piece in [(k, exchanged(part, axis, k)) for k in (2, 1, 3)] + [(0, part)]:
        out = lax.dynamic_update_index_in_dim(out, piece, me ^ k, 0)
    return out


def spread(part, axes):
    n = math.prod(lax.axis_size(a) for a in axes)
    return lax.all_to_all(jnp.broadcast_to(part[None], (n, *part.shape)), axes, 0, 0)


def summed_everywhere(value):
    rows, width = value.shape
    half = rows // 2
    first = value[:half].reshape(4, -1, width)
    second = value[half:].reshape(4, -1, width)
    first = scattered_sum(first, X)
    second = scattered_sum(second, Y)
    first = scattered_sum(first.reshape(4, -1, width), Y)
    second = scattered_sum(second.reshape(4, -1, width), X)
    n = lax.axis_size(Z)
    both = jnp.concatenate(
        [first.reshape(n, -1, width), second.reshape(n, -1, width)], 1
    )
    mine = lax.all_to_all(both, Z, 0, 0).sum(0)
    both = spread(mine, (Z,))
    at = both.shape[1] // 2
    first = both[:, :at].reshape(-1, width)
    second = both[:, at:].reshape(-1, width)
    first = gathered(first, Y).reshape(-1, width)
    second = gathered(second, X).reshape(-1, width)
    first = gathered(first, X).reshape(-1, width)
    second = gathered(second, Y).reshape(-1, width)
    return jnp.concatenate([first, second], 0)


def merged(stats, axes):
    pieces = spread(stats, axes)
    logs = pieces[:, :2]
    top = logs.max(0)
    factor = jnp.exp(logs - top)
    total = factor.sum(0)
    mean = (factor[:, 1] * pieces[:, 2]).sum(0) / total[1]
    return jnp.concatenate([top + jnp.log(total), mean[None]], 0)


def local(queries, queue, mentor_logit_grid, positives):
    row_count = queries.shape[0]
    key_count = queue.shape[0]
    score_scale = score_factor / math.sqrt(queries.shape[1])
    scores = score_scale * jnp.einsum(
        "rd,kd->rk", queries, queue, preferred_element_type=jnp.float32
    )
    key_index = lax.axis_index(QUEUE) * key_count + jnp.arange(key_count, dtype=jnp.int32)
    positive_match = (key_index[None, :] == positives[:, None]).astype(jnp.float32)
    mentor_model = mentor_logit_grid.astype(jnp.float32) + reward_value * positive_match
    stud_max = jnp.max(scores, axis=1)
    stud_sum = jnp.sum(jnp.exp(scores - stud_max[:, None]), axis=1)
    teach_max = jnp.max(mentor_model, axis=1)
    teach_exp = jnp.exp(mentor_model - teach_max[:, None])
    teach_sum = jnp.sum(teach_exp, axis=1)
    cross_sum = jnp.sum(teach_exp * (mentor_model - scores), axis=1)
    stats = jnp.stack(
        [
            (stud_max + jnp.log(stud_sum)).reshape(8, -1),
            (teach_max + jnp.log(teach_sum)).reshape(8, -1),
            (cross_sum / teach_sum).reshape(8, -1),
        ]
    )
    stud_log, teach_log, cross = merged(merged(stats, (X, Y)), (Z,))
    divergence = jnp.sum(cross - teach_log + stud_log)
    stud_log = stud_log.reshape(-1)
    teach_log = teach_log.reshape(-1)
    weights = (
        jnp.exp(scores - stud_log[:, None]) - jnp.exp(mentor_model - teach_log[:, None])
    ).astype(jnp.bfloat16)
    partial_value = jnp.dot(weights, queue, preferred_element_type=jnp.float32)
    query_grad = summed_everywhere(partial_value)
    loss_total = divergence + lax.ppermute(divergence, "batch", [(0, 1), (1, 0)])
    loss_value = loss_total / (row_count * lax.axis_size("batch"))
    return (query_grad, loss_value)


def solution(mesh):
    finer = Mesh(
        mesh.devices.reshape(mesh.shape["batch"], 4, 4, 8),
        ("batch", X, Y, Z),
    )
    return jax.shard_map(
        local,
        mesh=finer,
        in_specs=(P("batch", None), P(QUEUE, None), P("batch", QUEUE), P("batch")),
        out_specs=(P("batch", None), P()),
        check_vma=False,
    )
```

```python
import functools
import math

import jax
import jax.numpy as jnp
from jax import lax
from jax.experimental import pallas as pl
from jax.experimental.pallas import tpu as pltpu
from jax.sharding import Mesh
from jax.sharding import PartitionSpec as P

X, Y, Z = "queue_0", "queue_1", "queue_2"
QUEUE = (X, Y, Z)

score_factor = 3.0
reward_value = 12.0


def exchanged(part, axis, k):
    n = lax.axis_size(axis)
    return lax.ppermute(part, axis, [(i, i ^ k) for i in range(n)])


SHARE_LIMIT = 56 * 1024 * 1024
SMALL_LIMIT = 16 * 1024 * 1024

BLOCK = 128
TILE = 512
LIMIT = 60 * 1024 * 1024
ORDER = (2, 1, 3)


def as_column(row):
    return jnp.broadcast_to(row, (BLOCK, BLOCK)).T[:, :1]


def teacher_logits(mentor, wanted):
    column = lax.broadcasted_iota(jnp.int32, mentor.shape, 1)
    return mentor.astype(jnp.float32) + jnp.where(column == wanted, reward_value, 0.0)


def stats_kernel(
    base_ref, queries_ref, queue_ref, mentor_ref, positives_ref, scores_ref, sent_ref
):
    step = pl.program_id(0)
    scale = score_factor / math.sqrt(queries_ref.shape[1])
    tile = scale * lax.dot_general(
        queries_ref[...], queue_ref[...], (((1,), (1,)), ((), ())),
        preferred_element_type=jnp.float32,
    )
    scores_ref[...] = tile
    for part in range(TILE // BLOCK):
        at = slice(part * BLOCK, (part + 1) * BLOCK)
        number = step * (TILE // BLOCK) + part
        scores = tile[at, :]
        stud_max = jnp.max(scores, axis=1, keepdims=True)
        stud_sum = jnp.sum(jnp.exp(scores - stud_max), axis=1, keepdims=True)
        wanted = as_column(positives_ref[pl.ds(number, 1), :]) - base_ref[0]
        teacher = teacher_logits(mentor_ref[at, :], wanted)
        teach_max = jnp.max(teacher, axis=1, keepdims=True)
        teach_exp = jnp.exp(teacher - teach_max)
        teach_sum = jnp.sum(teach_exp, axis=1, keepdims=True)
        cross_sum = jnp.sum(teach_exp * (teacher - scores), axis=1, keepdims=True)
        lane = lax.broadcasted_iota(jnp.int32, (BLOCK, BLOCK), 1)
        packed = jnp.zeros((BLOCK, BLOCK), jnp.float32)
        for k, column in enumerate((stud_max, stud_sum, teach_max, teach_sum, cross_sum)):
            packed = jnp.where(lane == k, column, packed)
        rows = packed.T
        stud_max, stud_sum = rows[0:1, :], rows[1:2, :]
        teach_max, teach_sum, cross_sum = rows[2:3, :], rows[3:4, :], rows[4:5, :]
        sent = (stud_max, stud_sum, teach_max + jnp.log(teach_sum), cross_sum / teach_sum)
        for k, row in enumerate(sent):
            sent_ref[:, pl.ds(8 * k + number, 1), :] = jnp.broadcast_to(
                row[None], (sent_ref.shape[0], 1, BLOCK)
            )


def local_stats(base, queries, queue, mentor, positives, copies):
    rows, width = queries.shape
    keys = queue.shape[0]
    return pl.pallas_call(
        stats_kernel,
        grid=(rows // TILE,),
        in_specs=[
            pl.BlockSpec(memory_space=pltpu.SMEM),
            pl.BlockSpec((TILE, width), lambda i: (i, 0)),
            pl.BlockSpec((keys, width), lambda i: (0, 0)),
            pl.BlockSpec((TILE, keys), lambda i: (i, 0)),
            pl.BlockSpec((8, BLOCK), lambda i: (0, 0)),
        ],
        out_specs=[
            pl.BlockSpec((TILE, keys), lambda i: (i, 0)),
            pl.BlockSpec((copies, 32, BLOCK), lambda i: (0, 0, 0)),
        ],
        out_shape=[
            jax.ShapeDtypeStruct((rows, keys), jnp.float32),
            jax.ShapeDtypeStruct((copies, 32, BLOCK), jnp.float32),
        ],
        compiler_params=pltpu.CompilerParams(vmem_limit_bytes=LIMIT),
        name="local_stats",
    )(base, queries, queue, mentor, positives)


def merge(pieces):
    tops, totals, logs, means = (pieces[:, 8 * k : 8 * k + 8] for k in range(4))
    stud_top = tops.max(0)
    stud_total = (totals * jnp.exp(tops - stud_top)).sum(0)
    teach_top = logs.max(0)
    factor = jnp.exp(logs - teach_top)
    total = factor.sum(0)
    return stud_top, stud_total, teach_top + jnp.log(total), (factor * means).sum(0) / total


def merge_kernel(pieces_ref, out_ref):
    for k, value in enumerate(merge(pieces_ref[...])):
        out_ref[:, 8 * k : 8 * k + 8, :] = jnp.broadcast_to(
            value[None], (out_ref.shape[0], 8, BLOCK)
        )


def logs_kernel(pieces_ref, logs_ref, total_ref):
    stud_top, stud_total, teach_log, cross = merge(pieces_ref[...])
    stud_log = stud_top + jnp.log(stud_total)
    logs_ref[0:8, :] = stud_log
    logs_ref[8:16, :] = teach_log
    total = jnp.sum(cross - teach_log + stud_log)
    total_ref[...] = jnp.broadcast_to(total, total_ref.shape)


def share_kernel(count, numbers_ref, base_ref, logs_ref, positives_ref, *refs):
    scores, mentor = refs[:count], refs[count : 2 * count]
    queue_ref, outs, weights_ref = refs[2 * count], refs[2 * count + 1 : -1], refs[-1]

    @pl.when(pl.program_id(0) == 0)
    def _():
        for k in range(count):
            number = numbers_ref[k]
            stud_log = as_column(logs_ref[pl.ds(number, 1), :])
            teach_log = as_column(logs_ref[pl.ds(8 + number, 1), :])
            wanted = as_column(positives_ref[pl.ds(number, 1), :]) - base_ref[0]
            weights = jnp.exp(scores[k][...] - stud_log) - jnp.exp(
                teacher_logits(mentor[k][...], wanted) - teach_log
            )
            weights_ref[k * BLOCK : (k + 1) * BLOCK, :] = weights.astype(jnp.bfloat16)

    out = jnp.dot(weights_ref[...], queue_ref[...], preferred_element_type=jnp.float32)
    for k in range(count):
        outs[k][...] = out[k * BLOCK : (k + 1) * BLOCK, :]


def shares(numbers, base, logs, positives, scores, mentor, queue):
    count = numbers.shape[0]
    keys, width = queue.shape
    part = 512

    def rows(k):
        return pl.BlockSpec((BLOCK, keys), lambda i, numbers, base: (numbers[k], 0))

    return pl.pallas_call(
        functools.partial(share_kernel, count),
        grid_spec=pltpu.PrefetchScalarGridSpec(
            num_scalar_prefetch=2,
            grid=(width // part,),
            in_specs=[
                pl.BlockSpec((16, BLOCK), lambda i, numbers, base: (0, 0)),
                pl.BlockSpec((8, BLOCK), lambda i, numbers, base: (0, 0)),
                *(rows(k) for k in range(count)),
                *(rows(k) for k in range(count)),
                pl.BlockSpec((keys, part), lambda i, numbers, base: (0, i)),
            ],
            out_specs=[pl.BlockSpec((BLOCK, part), lambda i, numbers, base: (0, i))] * count,
            scratch_shapes=[pltpu.VMEM((count * BLOCK, keys), jnp.bfloat16)],
        ),
        out_shape=[jax.ShapeDtypeStruct((BLOCK, width), jnp.float32)] * count,
        compiler_params=pltpu.CompilerParams(vmem_limit_bytes=SHARE_LIMIT),
        cost_estimate=pl.CostEstimate(flops=0, bytes_accessed=0, transcendentals=0),
        name="shares",
    )(numbers, base, logs, positives, *[scores] * count, *[mentor] * count, queue)


def split_kernel(me_ref, a, b, c, d, own_ref, *outs):
    rows = own_ref.shape[0]
    for k, out in zip((0, *ORDER), (own_ref, *outs)):
        at = pl.ds(pl.multiple_of((me_ref[0] ^ k) * rows, rows), rows)
        out[...] = (a[at, :] + b[at, :]) + (c[at, :] + d[at, :])


def split_sum(me, parts):
    rows, width = parts[0].shape
    whole = pl.BlockSpec(memory_space=pltpu.VMEM)
    return pl.pallas_call(
        split_kernel,
        in_specs=[pl.BlockSpec(memory_space=pltpu.SMEM), *[whole] * 4],
        out_specs=[whole] * 4,
        out_shape=[jax.ShapeDtypeStruct((rows // 4, width), jnp.float32)] * 4,
        compiler_params=pltpu.CompilerParams(vmem_limit_bytes=SMALL_LIMIT),
        name="split_sum",
    )(me, *parts)


def columns_kernel(*refs):
    out = refs[-1]
    rows = refs[0].shape[0]
    for half in range(2):
        a, b, c, d = (ref[...] for ref in refs[4 * half : 4 * half + 4])
        total = (a + b) + (c + d)
        for k in range(out.shape[0]):
            out[k, half * rows : (half + 1) * rows, :] = total[:, k * BLOCK : (k + 1) * BLOCK]


def column_blocks(first, second):
    rows, width = first[0].shape
    whole = pl.BlockSpec(memory_space=pltpu.VMEM)
    return pl.pallas_call(
        columns_kernel,
        in_specs=[whole] * 8,
        out_specs=whole,
        out_shape=jax.ShapeDtypeStruct((width // BLOCK, 2 * rows, BLOCK), jnp.float32),
        compiler_params=pltpu.CompilerParams(vmem_limit_bytes=SMALL_LIMIT),
        name="column_blocks",
    )(*first, *second)


def total_kernel(pieces_ref, out_ref):
    total = pieces_ref[...].sum(0)
    out_ref[...] = jnp.broadcast_to(total[None], out_ref.shape)


def rows_kernel(blocks_ref, first_ref, second_ref):
    rows = first_ref.shape[0]
    for k in range(blocks_ref.shape[0]):
        at = slice(k * BLOCK, (k + 1) * BLOCK)
        first_ref[:, at] = blocks_ref[k, :rows, :]
        second_ref[:, at] = blocks_ref[k, rows:, :]


def assemble_kernel(x_ref, y_ref, *refs):
    out, sem = refs[-2], refs[-1]
    rows = refs[0].shape[0]
    part = rows // 4
    copies = []
    for half, (outer, inner) in enumerate(((x_ref[0], y_ref[0]), (y_ref[0], x_ref[0]))):
        for i, k in enumerate((0, *ORDER)):
            for j, m in enumerate((0, *ORDER)):
                at = 4 * rows * half + (outer ^ k) * rows + (inner ^ m) * part
                copies.append(
                    pltpu.make_async_copy(
                        refs[4 * half + i].at[j * part : (j + 1) * part, :],
                        out.at[pl.ds(pl.multiple_of(at, part), part), :],
                        sem.at[len(copies)],
                    )
                )
    for copy in copies:
        copy.start()
    for copy in copies:
        copy.wait()


def assembled(x, y, first, second):
    rows, width = first[0].shape
    return pl.pallas_call(
        assemble_kernel,
        in_specs=[pl.BlockSpec(memory_space=pltpu.SMEM)] * 2
        + [pl.BlockSpec(memory_space=pl.ANY)] * 8,
        out_specs=pl.BlockSpec(memory_space=pl.ANY),
        out_shape=jax.ShapeDtypeStruct((8 * rows, width), jnp.float32),
        scratch_shapes=[pltpu.SemaphoreType.DMA((32,))],
        compiler_params=pltpu.CompilerParams(vmem_limit_bytes=SMALL_LIMIT),
        name="assembled",
    )(x, y, *first, *second)


def received(part, axis):
    return [exchanged(part, axis, k) for k in ORDER]


def local(queries, queue, mentor_logit_grid, positives):
    row_count = queries.shape[0]
    key_count = queue.shape[0]
    whole = pl.BlockSpec(memory_space=pltpu.VMEM)
    x, y = (lax.axis_index(axis).astype(jnp.int32) for axis in (X, Y))
    base = (lax.axis_index(QUEUE) * key_count).astype(jnp.int32).reshape(1)
    positives = positives.reshape(8, BLOCK)
    scores, sent = local_stats(base, queries, queue, mentor_logit_grid, positives, 16)
    pieces = lax.all_to_all(sent, (X, Y), 0, 0)
    sent = pl.pallas_call(
        merge_kernel,
        out_shape=jax.ShapeDtypeStruct((8, 32, BLOCK), jnp.float32),
        name="merge_plane",
    )(pieces)
    pieces = lax.all_to_all(sent, Z, 0, 0)
    logs, divergence = pl.pallas_call(
        logs_kernel,
        out_shape=[
            jax.ShapeDtypeStruct((16, BLOCK), jnp.float32),
            jax.ShapeDtypeStruct((8, BLOCK), jnp.float32),
        ],
        name="merge_all",
    )(pieces)

    def share(partners):
        numbers = jnp.stack([n for k in partners for n in (x ^ k, 4 + (y ^ k))])
        return shares(numbers, base, logs, positives, scores, mentor_logit_grid, queue)

    early = share(ORDER[:1])
    late = share((*ORDER[1:], 0))
    sent = [*early, *late]
    first = [sent[6]] + [exchanged(sent[2 * i], X, k) for i, k in enumerate(ORDER)]
    second = [sent[7]] + [exchanged(sent[2 * i + 1], Y, k) for i, k in enumerate(ORDER)]
    first = split_sum(y.reshape(1), first)
    second = split_sum(x.reshape(1), second)
    first = [first[0]] + [exchanged(p, Y, k) for p, k in zip(first[1:], ORDER)]
    second = [second[0]] + [exchanged(p, X, k) for p, k in zip(second[1:], ORDER)]
    blocks = column_blocks(first, second)
    pieces = lax.all_to_all(blocks, Z, 0, 0)
    total = pl.pallas_call(
        total_kernel,
        out_shape=jax.ShapeDtypeStruct(pieces.shape, jnp.float32),
        name="total",
    )(pieces)
    blocks = lax.all_to_all(total, Z, 0, 0)
    rows, width = blocks.shape[1] // 2, queries.shape[1]
    first, second = pl.pallas_call(
        rows_kernel,
        out_shape=[jax.ShapeDtypeStruct((rows, width), jnp.float32)] * 2,
        name="row_blocks",
    )(blocks)
    first = jnp.concatenate([first, *received(first, Y)], 0)
    second = jnp.concatenate([second, *received(second, X)], 0)
    first = [first, *received(first, X)]
    second = [second, *received(second, Y)]
    query_grad = assembled(x.reshape(1), y.reshape(1), first, second)
    divergence = divergence[0, 0]
    loss_total = divergence + lax.ppermute(divergence, "batch", [(0, 1), (1, 0)])
    loss_value = loss_total / (row_count * lax.axis_size("batch"))
    return (query_grad, loss_value)


def solution(mesh):
    finer = Mesh(
        mesh.devices.reshape(mesh.shape["batch"], 4, 4, 8),
        ("batch", X, Y, Z),
    )
    return jax.shard_map(
        local,
        mesh=finer,
        in_specs=(P("batch", None), P(QUEUE, None), P("batch", QUEUE), P("batch")),
        out_specs=(P("batch", None), P()),
        check_vma=False,
    )
```

```python
import functools
import math

import jax
import jax.numpy as jnp
from jax import lax
from jax.experimental import pallas as pl
from jax.experimental.pallas import tpu as pltpu
from jax.sharding import Mesh
from jax.sharding import PartitionSpec as P

X, Y, Z = "queue_0", "queue_1", "queue_2"
QUEUE = (X, Y, Z)

score_factor = 3.0
reward_value = 12.0


def exchanged(part, axis, k):
    n = lax.axis_size(axis)
    return lax.ppermute(part, axis, [(i, i ^ k) for i in range(n)])


SHARE_LIMIT = 49 * 1024 * 1024
SMALL_LIMIT = 8 * 1024 * 1024

BLOCK = 128
PART = 32
TILE = 512
LIMIT = 60 * 1024 * 1024
ORDER = (2, 1, 3)
WHOLE = pl.BlockSpec(memory_space=pltpu.VMEM)


def as_column(row):
    return jnp.broadcast_to(row, (BLOCK, BLOCK)).T[:, :1]


def teacher_logits(mentor, wanted):
    column = lax.broadcasted_iota(jnp.int32, mentor.shape, 1)
    return mentor.astype(jnp.float32) + jnp.where(column == wanted, reward_value, 0.0)


def stats_kernel(
    base_ref, queries_ref, queue_ref, mentor_ref, positives_ref, logits_ref, sent_ref
):
    step = pl.program_id(0)
    scale = score_factor / math.sqrt(queries_ref.shape[1])
    tile = scale * lax.dot_general(
        queries_ref[...], queue_ref[...], (((1,), (1,)), ((), ())),
        preferred_element_type=jnp.float32,
    )
    logits_ref[0] = tile
    for part in range(TILE // BLOCK):
        at = slice(part * BLOCK, (part + 1) * BLOCK)
        number = step * (TILE // BLOCK) + part
        scores = tile[at, :]
        stud_max = jnp.max(scores, axis=1, keepdims=True)
        stud_sum = jnp.sum(jnp.exp(scores - stud_max), axis=1, keepdims=True)
        wanted = as_column(positives_ref[pl.ds(number, 1), :]) - base_ref[0]
        teacher = teacher_logits(mentor_ref[at, :], wanted)
        logits_ref[1, at, :] = teacher
        teach_max = jnp.max(teacher, axis=1, keepdims=True)
        teach_exp = jnp.exp(teacher - teach_max)
        teach_sum = jnp.sum(teach_exp, axis=1, keepdims=True)
        cross_sum = jnp.sum(teach_exp * (teacher - scores), axis=1, keepdims=True)
        lane = lax.broadcasted_iota(jnp.int32, (BLOCK, BLOCK), 1)
        packed = jnp.zeros((BLOCK, BLOCK), jnp.float32)
        for k, column in enumerate((stud_max, stud_sum, teach_max, teach_sum, cross_sum)):
            packed = jnp.where(lane == k, column, packed)
        rows = packed.T
        stud_max, stud_sum = rows[0:1, :], rows[1:2, :]
        teach_max, teach_sum, cross_sum = rows[2:3, :], rows[3:4, :], rows[4:5, :]
        sent = (stud_max, stud_sum, teach_max + jnp.log(teach_sum), cross_sum / teach_sum)
        for k, row in enumerate(sent):
            sent_ref[:, pl.ds(8 * k + number, 1), :] = jnp.broadcast_to(
                row[None], (sent_ref.shape[0], 1, BLOCK)
            )


def local_stats(base, queries, queue, mentor, positives, copies):
    rows, width = queries.shape
    keys = queue.shape[0]
    return pl.pallas_call(
        stats_kernel,
        grid=(rows // TILE,),
        in_specs=[
            pl.BlockSpec(memory_space=pltpu.SMEM),
            pl.BlockSpec((TILE, width), lambda i: (i, 0)),
            pl.BlockSpec((keys, width), lambda i: (0, 0)),
            pl.BlockSpec((TILE, keys), lambda i: (i, 0)),
            pl.BlockSpec((8, BLOCK), lambda i: (0, 0)),
        ],
        out_specs=[
            pl.BlockSpec((2, TILE, keys), lambda i: (0, i, 0)),
            pl.BlockSpec((copies, 32, BLOCK), lambda i: (0, 0, 0)),
        ],
        out_shape=[
            jax.ShapeDtypeStruct((2, rows, keys), jnp.float32),
            jax.ShapeDtypeStruct((copies, 32, BLOCK), jnp.float32),
        ],
        compiler_params=pltpu.CompilerParams(vmem_limit_bytes=LIMIT),
        name="local_stats",
    )(base, queries, queue, mentor, positives)


def merge(pieces):
    tops, totals, logs, means = (pieces[:, 8 * k : 8 * k + 8] for k in range(4))
    stud_top = tops.max(0)
    stud_total = (totals * jnp.exp(tops - stud_top)).sum(0)
    teach_top = logs.max(0)
    factor = jnp.exp(logs - teach_top)
    total = factor.sum(0)
    return stud_top, stud_total, teach_top + jnp.log(total), (factor * means).sum(0) / total


def merge_kernel(pieces_ref, out_ref):
    for k, value in enumerate(merge(pieces_ref[...])):
        out_ref[:, 8 * k : 8 * k + 8, :] = jnp.broadcast_to(
            value[None], (out_ref.shape[0], 8, BLOCK)
        )


def logs_kernel(pieces_ref, logs_ref, total_ref):
    stud_top, stud_total, teach_log, cross = merge(pieces_ref[...])
    stud_log = stud_top + jnp.log(stud_total)
    logs_ref[0:8, :] = stud_log
    logs_ref[8:16, :] = teach_log
    total = jnp.sum(cross - teach_log + stud_log)
    total_ref[...] = jnp.broadcast_to(total, total_ref.shape)


def share_kernel(numbers_ref, logs_ref, queue_ref, logits_hbm, *refs):
    outs, (logits_ref, weights_ref, sem) = refs[:-3], refs[-3:]
    copies = []
    for k in range(numbers_ref.shape[0]):
        at = pl.ds(pl.multiple_of(numbers_ref[k] * BLOCK, BLOCK), BLOCK)
        copies.append(
            pltpu.make_async_copy(logits_hbm.at[:, at, :], logits_ref.at[k], sem.at[k])
        )
        copies[k].start()
    for k, copy in enumerate(copies):
        number = numbers_ref[k]
        stud_log = as_column(logs_ref[pl.ds(number, 1), :])
        teach_log = as_column(logs_ref[pl.ds(8 + number, 1), :])
        copy.wait()
        weights = jnp.exp(logits_ref[k, 0] - stud_log) - jnp.exp(logits_ref[k, 1] - teach_log)
        weights_ref[k * BLOCK : (k + 1) * BLOCK, :] = weights.astype(jnp.bfloat16)
    total = jnp.dot(weights_ref[...], queue_ref[...], preferred_element_type=jnp.float32)
    rows = outs[0].shape[0]
    for k, out in enumerate(outs):
        out[...] = total[k * rows : (k + 1) * rows, :]


def shares(numbers, parts, logs, queue, logits):
    count = numbers.shape[0]
    keys, width = queue.shape
    out = jax.ShapeDtypeStruct((BLOCK // parts, width), jnp.float32)
    return pl.pallas_call(
        share_kernel,
        in_specs=[
            pl.BlockSpec(memory_space=pltpu.SMEM), WHOLE, WHOLE,
            pl.BlockSpec(memory_space=pl.ANY),
        ],
        out_specs=[WHOLE] * (count * parts),
        out_shape=[out] * (count * parts),
        scratch_shapes=[
            pltpu.VMEM((count, 2, BLOCK, keys), jnp.float32),
            pltpu.VMEM((count * BLOCK, keys), jnp.bfloat16),
            pltpu.SemaphoreType.DMA((count,)),
        ],
        compiler_params=pltpu.CompilerParams(vmem_limit_bytes=SHARE_LIMIT),
        cost_estimate=pl.CostEstimate(flops=0, bytes_accessed=0, transcendentals=0),
        name="shares",
    )(numbers, logs, queue, logits)


def relay_kernel(*refs):
    for k in range(4):
        block, half, out = refs[k], refs[4 + k], refs[8 + k]
        rows = half.shape[0]
        out[...] = block[...]
        at = slice(rows, 2 * rows) if k % 2 == 0 else slice(0, rows)
        out[at, :] = block[at, :] + half[...]


def relayed(blocks, halves):
    return pl.pallas_call(
        relay_kernel,
        in_specs=[WHOLE] * 8,
        out_specs=[WHOLE] * 4,
        out_shape=[jax.ShapeDtypeStruct(b.shape, b.dtype) for b in blocks],
        compiler_params=pltpu.CompilerParams(vmem_limit_bytes=SMALL_LIMIT),
        name="relayed",
    )(*blocks, *halves)


def split_kernel(*refs):
    places, parts, outs = refs[:2], refs[2:8], refs[8:]
    rows = outs[0].shape[0]
    for half in range(2):
        a, b, c = parts[3 * half : 3 * half + 3]
        for i, k in enumerate((0, *ORDER)):
            at = pl.ds(pl.multiple_of((places[half][0] ^ k) * rows, rows), rows)
            outs[4 * half + i][...] = a[at, :] + (b[at, :] + c[at, :])


def split_sums(places, first, second):
    rows, width = first[0].shape
    outs = pl.pallas_call(
        split_kernel,
        in_specs=[pl.BlockSpec(memory_space=pltpu.SMEM)] * 2 + [WHOLE] * 6,
        out_specs=[WHOLE] * 8,
        out_shape=[jax.ShapeDtypeStruct((rows // 4, width), jnp.float32)] * 8,
        compiler_params=pltpu.CompilerParams(vmem_limit_bytes=SMALL_LIMIT),
        name="split_sums",
    )(*places, *first, *second)
    return outs[:4], outs[4:]


def columns_kernel(*refs):
    out = refs[-1]
    rows = refs[0].shape[0]
    for half in range(2):
        a, b, c, d = (ref[...] for ref in refs[4 * half : 4 * half + 4])
        total = (a + b) + (c + d)
        for k in range(out.shape[0]):
            out[k, half * rows : (half + 1) * rows, :] = total[:, k * BLOCK : (k + 1) * BLOCK]


def column_blocks(first, second):
    rows, width = first[0].shape
    return pl.pallas_call(
        columns_kernel,
        in_specs=[WHOLE] * 8,
        out_specs=WHOLE,
        out_shape=jax.ShapeDtypeStruct((width // BLOCK, 2 * rows, BLOCK), jnp.float32),
        compiler_params=pltpu.CompilerParams(vmem_limit_bytes=SMALL_LIMIT),
        name="column_blocks",
    )(*first, *second)


def total_kernel(pieces_ref, out_ref):
    total = pieces_ref[...].sum(0)
    out_ref[...] = jnp.broadcast_to(total[None], out_ref.shape)


def rows_kernel(blocks_ref, first_ref, second_ref):
    rows = first_ref.shape[0]
    for k in range(blocks_ref.shape[0]):
        at = slice(k * BLOCK, (k + 1) * BLOCK)
        first_ref[:, at] = blocks_ref[k, :rows, :]
        second_ref[:, at] = blocks_ref[k, rows:, :]


def stack_kernel(*refs):
    rows = refs[0].shape[0]
    for half, out in enumerate(refs[8:]):
        for k in range(4):
            out[k * rows : (k + 1) * rows, :] = refs[4 * half + k][...]


def stacked(first, second):
    rows, width = first[0].shape
    return pl.pallas_call(
        stack_kernel,
        in_specs=[WHOLE] * 8,
        out_specs=[WHOLE] * 2,
        out_shape=[jax.ShapeDtypeStruct((4 * rows, width), jnp.float32)] * 2,
        compiler_params=pltpu.CompilerParams(vmem_limit_bytes=SMALL_LIMIT),
        name="stacked",
    )(*first, *second)


def halves_kernel(a, b, c, d, *outs):
    for k, ref in enumerate((a, b, c, d)):
        rows = ref.shape[0] // 2
        outs[k][...] = ref[:rows, :] if k % 2 == 0 else ref[rows:, :]


def halves(blocks):
    rows, width = blocks[0].shape
    return pl.pallas_call(
        halves_kernel,
        in_specs=[WHOLE] * 4,
        out_specs=[WHOLE] * 4,
        out_shape=[jax.ShapeDtypeStruct((rows // 2, width), jnp.float32)] * 4,
        compiler_params=pltpu.CompilerParams(vmem_limit_bytes=SMALL_LIMIT),
        name="halves",
    )(*blocks)


def assemble_kernel(kinds, x_ref, y_ref, *refs):
    out, sem = refs[-2], refs[-1]
    places = (x_ref[0], y_ref[0]), (y_ref[0], x_ref[0])
    copies = []
    for (half, k, start), ref in zip(kinds, refs):
        outer, inner = places[half]
        for j in range(ref.shape[0] // PART):
            at = 4 * BLOCK * half + (outer ^ k) * BLOCK + (inner ^ (0, *ORDER)[start + j]) * PART
            copies.append(
                pltpu.make_async_copy(
                    ref.at[j * PART : (j + 1) * PART, :],
                    out.at[pl.ds(pl.multiple_of(at, PART), PART), :],
                    sem.at[len(copies)],
                )
            )
    for copy in copies:
        copy.start()
    for copy in copies:
        copy.wait()


def assembled(kinds, pieces, earlier, x, y):
    count = sum(piece.shape[0] for piece in pieces) // PART
    kept = [] if earlier is None else [earlier]
    return pl.pallas_call(
        functools.partial(assemble_kernel, kinds),
        in_specs=[pl.BlockSpec(memory_space=pltpu.SMEM)] * 2
        + [WHOLE] * len(pieces)
        + [pl.BlockSpec(memory_space=pl.ANY)] * len(kept),
        out_specs=pl.BlockSpec(memory_space=pl.ANY),
        out_shape=jax.ShapeDtypeStruct((8 * BLOCK, pieces[0].shape[1]), jnp.float32),
        scratch_shapes=[pltpu.SemaphoreType.DMA((count,))],
        input_output_aliases={2 + len(pieces): 0} if kept else {},
        compiler_params=pltpu.CompilerParams(vmem_limit_bytes=SMALL_LIMIT),
        name="assembled",
    )(x, y, *pieces, *kept)


def received(part, axis):
    return {k: exchanged(part, axis, k) for k in reversed(ORDER)}


def local(queries, queue, mentor_logit_grid, positives):
    row_count = queries.shape[0]
    key_count = queue.shape[0]
    x, y = (lax.axis_index(axis).astype(jnp.int32) for axis in (X, Y))
    base = (lax.axis_index(QUEUE) * key_count).astype(jnp.int32).reshape(1)
    positives = positives.reshape(8, BLOCK)
    logits, sent = local_stats(base, queries, queue, mentor_logit_grid, positives, 16)
    pieces = lax.all_to_all(sent, (X, Y), 0, 0)
    sent = pl.pallas_call(
        merge_kernel,
        in_specs=[WHOLE],
        out_specs=WHOLE,
        out_shape=jax.ShapeDtypeStruct((8, 32, BLOCK), jnp.float32),
        compiler_params=pltpu.CompilerParams(vmem_limit_bytes=SMALL_LIMIT),
        name="merge_plane",
    )(pieces)
    pieces = lax.all_to_all(sent, Z, 0, 0)
    logs, divergence = pl.pallas_call(
        logs_kernel,
        in_specs=[WHOLE],
        out_specs=[WHOLE] * 2,
        out_shape=[
            jax.ShapeDtypeStruct((16, BLOCK), jnp.float32),
            jax.ShapeDtypeStruct((1, 1), jnp.float32),
        ],
        compiler_params=pltpu.CompilerParams(vmem_limit_bytes=SMALL_LIMIT),
        name="merge_all",
    )(pieces)

    def share(partners, parts=1):
        numbers = jnp.stack([n for k in partners for n in (x ^ k, 4 + (y ^ k))])
        return shares(numbers, parts, logs, queue, logits)

    far = share((2,), 2)
    ways = (X, 1), (X, 3), (Y, 1), (Y, 3)
    came = [exchanged(part, *way) for part, way in zip(far, ways)]
    one = share((1, 3))
    blocks = [one[0], one[2], one[1], one[3]]
    blocks = relayed(blocks, [came[1], came[0], came[3], came[2]])
    got = [exchanged(block, *way) for block, way in zip(blocks, ways)]
    own = share((0,))
    places = y.reshape(1), x.reshape(1)
    first, second = split_sums(places, [own[0], *got[:2]], [own[1], *got[2:]])
    first = [first[0]] + [exchanged(p, Y, k) for p, k in zip(first[1:], ORDER)]
    second = [second[0]] + [exchanged(p, X, k) for p, k in zip(second[1:], ORDER)]
    blocks = column_blocks(first, second)
    pieces = lax.all_to_all(blocks, Z, 0, 0)
    total = pl.pallas_call(
        total_kernel,
        in_specs=[WHOLE],
        out_specs=WHOLE,
        out_shape=jax.ShapeDtypeStruct(pieces.shape, jnp.float32),
        compiler_params=pltpu.CompilerParams(vmem_limit_bytes=SMALL_LIMIT),
        name="total",
    )(pieces)
    blocks = lax.all_to_all(total, Z, 0, 0)
    rows, width = blocks.shape[1] // 2, queries.shape[1]
    first, second = pl.pallas_call(
        rows_kernel,
        in_specs=[WHOLE],
        out_specs=[WHOLE] * 2,
        out_shape=[jax.ShapeDtypeStruct((rows, width), jnp.float32)] * 2,
        compiler_params=pltpu.CompilerParams(vmem_limit_bytes=SMALL_LIMIT),
        name="row_blocks",
    )(blocks)
    from_y, from_x = received(first, Y), received(second, X)
    first, second = stacked(
        [first, *(from_y[k] for k in ORDER)], [second, *(from_x[k] for k in ORDER)]
    )
    blocks = [exchanged(first, X, 1), exchanged(first, X, 3)]
    blocks += [exchanged(second, Y, 1), exchanged(second, Y, 3)]
    upper_x, lower_x, upper_y, lower_y = halves([blocks[1], blocks[0], blocks[3], blocks[2]])
    far = [exchanged(upper_x, X, 1), exchanged(lower_x, X, 3)]
    far += [exchanged(upper_y, Y, 1), exchanged(lower_y, Y, 3)]
    places = x.reshape(1), y.reshape(1)
    kinds = (0, 0, 0), (1, 0, 0), (0, 1, 0), (0, 3, 0), (1, 1, 0), (1, 3, 0)
    query_grad = assembled(kinds, [first, second, *blocks], None, *places)
    kinds = (0, 2, 0), (0, 2, 2), (1, 2, 0), (1, 2, 2)
    query_grad = assembled(kinds, far, query_grad, *places)
    divergence = divergence[0, 0]
    loss_total = divergence + lax.ppermute(divergence, "batch", [(0, 1), (1, 0)])
    loss_value = loss_total / (row_count * lax.axis_size("batch"))
    return (query_grad, loss_value)


def solution(mesh):
    finer = Mesh(
        mesh.devices.reshape(mesh.shape["batch"], 4, 4, 8),
        ("batch", X, Y, Z),
    )
    return jax.shard_map(
        local,
        mesh=finer,
        in_specs=(P("batch", None), P(QUEUE, None), P("batch", QUEUE), P("batch")),
        out_specs=(P("batch", None), P()),
        check_vma=False,
    )
```

```python
import functools
import math

import jax
import jax.numpy as jnp
from jax import lax
from jax.experimental import pallas as pl
from jax.experimental.pallas import tpu as pltpu
from jax.sharding import Mesh
from jax.sharding import PartitionSpec as P

X, Y, Z = "queue_0", "queue_1", "queue_2"
QUEUE = (X, Y, Z)

score_factor = 3.0
reward_value = 12.0


def exchanged(part, axis, k):
    n = lax.axis_size(axis)
    return lax.ppermute(part, axis, [(i, i ^ k) for i in range(n)])


SHARE_LIMIT = 49 * 1024 * 1024
SMALL_LIMIT = 8 * 1024 * 1024

BLOCK = 128
PART = 32
TILE = 512
LIMIT = 60 * 1024 * 1024
ORDER = (2, 1, 3)
WHOLE = pl.BlockSpec(memory_space=pltpu.VMEM)


def moved(size, flops=0):
    return pl.CostEstimate(flops=flops, bytes_accessed=size, transcendentals=0)


def as_column(row):
    return jnp.broadcast_to(row, (BLOCK, BLOCK)).T[:, :1]


def teacher_logits(mentor, wanted):
    column = lax.broadcasted_iota(jnp.int32, mentor.shape, 1)
    return mentor.astype(jnp.float32) + jnp.where(column == wanted, reward_value, 0.0)


def stats_kernel(
    base_ref, queries_ref, queue_ref, mentor_ref, positives_ref, logits_ref, sent_ref
):
    step = pl.program_id(0)
    scale = score_factor / math.sqrt(queries_ref.shape[1])
    tile = scale * lax.dot_general(
        queries_ref[...], queue_ref[...], (((1,), (1,)), ((), ())),
        preferred_element_type=jnp.float32,
    )
    logits_ref[0] = tile
    for part in range(TILE // BLOCK):
        at = slice(part * BLOCK, (part + 1) * BLOCK)
        number = step * (TILE // BLOCK) + part
        scores = tile[at, :]
        stud_max = jnp.max(scores, axis=1, keepdims=True)
        stud_sum = jnp.sum(jnp.exp(scores - stud_max), axis=1, keepdims=True)
        wanted = as_column(positives_ref[pl.ds(number, 1), :]) - base_ref[0]
        teacher = teacher_logits(mentor_ref[at, :], wanted)
        logits_ref[1, at, :] = teacher
        teach_max = jnp.max(teacher, axis=1, keepdims=True)
        teach_exp = jnp.exp(teacher - teach_max)
        teach_sum = jnp.sum(teach_exp, axis=1, keepdims=True)
        cross_sum = jnp.sum(teach_exp * (teacher - scores), axis=1, keepdims=True)
        lane = lax.broadcasted_iota(jnp.int32, (BLOCK, BLOCK), 1)
        packed = jnp.zeros((BLOCK, BLOCK), jnp.float32)
        for k, column in enumerate((stud_max, stud_sum, teach_max, teach_sum, cross_sum)):
            packed = jnp.where(lane == k, column, packed)
        rows = packed.T
        stud_max, stud_sum = rows[0:1, :], rows[1:2, :]
        teach_max, teach_sum, cross_sum = rows[2:3, :], rows[3:4, :], rows[4:5, :]
        sent = (stud_max, stud_sum, teach_max + jnp.log(teach_sum), cross_sum / teach_sum)
        for k, row in enumerate(sent):
            sent_ref[:, pl.ds(8 * k + number, 1), :] = jnp.broadcast_to(
                row[None], (sent_ref.shape[0], 1, BLOCK)
            )


def local_stats(base, queries, queue, mentor, positives, copies):
    rows, width = queries.shape
    keys = queue.shape[0]
    return pl.pallas_call(
        stats_kernel,
        grid=(rows // TILE,),
        in_specs=[
            pl.BlockSpec(memory_space=pltpu.SMEM),
            pl.BlockSpec((TILE, width), lambda i: (i, 0)),
            pl.BlockSpec((keys, width), lambda i: (0, 0)),
            pl.BlockSpec((TILE, keys), lambda i: (i, 0)),
            pl.BlockSpec((8, BLOCK), lambda i: (0, 0)),
        ],
        out_specs=[
            pl.BlockSpec((2, TILE, keys), lambda i: (0, i, 0)),
            pl.BlockSpec((copies, 32, BLOCK), lambda i: (0, 0, 0)),
        ],
        out_shape=[
            jax.ShapeDtypeStruct((2, rows, keys), jnp.float32),
            jax.ShapeDtypeStruct((copies, 32, BLOCK), jnp.float32),
        ],
        compiler_params=pltpu.CompilerParams(vmem_limit_bytes=LIMIT),
        name="local_stats",
    )(base, queries, queue, mentor, positives)


def merge(pieces):
    tops, totals, logs, means = (pieces[:, 8 * k : 8 * k + 8] for k in range(4))
    stud_top = tops.max(0)
    stud_total = (totals * jnp.exp(tops - stud_top)).sum(0)
    teach_top = logs.max(0)
    factor = jnp.exp(logs - teach_top)
    total = factor.sum(0)
    return stud_top, stud_total, teach_top + jnp.log(total), (factor * means).sum(0) / total


def merge_kernel(pieces_ref, out_ref):
    for k, value in enumerate(merge(pieces_ref[...])):
        out_ref[:, 8 * k : 8 * k + 8, :] = jnp.broadcast_to(
            value[None], (out_ref.shape[0], 8, BLOCK)
        )


def logs_kernel(pieces_ref, logs_ref, total_ref):
    stud_top, stud_total, teach_log, cross = merge(pieces_ref[...])
    stud_log = stud_top + jnp.log(stud_total)
    logs_ref[0:8, :] = stud_log
    logs_ref[8:16, :] = teach_log
    total = jnp.sum(cross - teach_log + stud_log)
    total_ref[...] = jnp.broadcast_to(total, total_ref.shape)


def share_kernel(numbers_ref, logs_ref, queue_ref, logits_hbm, *refs):
    outs, (logits_ref, weights_ref, sem) = refs[:-3], refs[-3:]
    copies = []
    for k in range(numbers_ref.shape[0]):
        at = pl.ds(pl.multiple_of(numbers_ref[k] * BLOCK, BLOCK), BLOCK)
        copies.append(
            pltpu.make_async_copy(logits_hbm.at[:, at, :], logits_ref.at[k], sem.at[k])
        )
        copies[k].start()
    for k, copy in enumerate(copies):
        number = numbers_ref[k]
        stud_log = as_column(logs_ref[pl.ds(number, 1), :])
        teach_log = as_column(logs_ref[pl.ds(8 + number, 1), :])
        copy.wait()
        weights = jnp.exp(logits_ref[k, 0] - stud_log) - jnp.exp(logits_ref[k, 1] - teach_log)
        weights_ref[k * BLOCK : (k + 1) * BLOCK, :] = weights.astype(jnp.bfloat16)
    total = jnp.dot(weights_ref[...], queue_ref[...], preferred_element_type=jnp.float32)
    rows = outs[0].shape[0]
    for k, out in enumerate(outs):
        out[...] = total[k * rows : (k + 1) * rows, :]


def shares(numbers, parts, logs, queue, logits):
    count = numbers.shape[0]
    keys, width = queue.shape
    out = jax.ShapeDtypeStruct((BLOCK // parts, width), jnp.float32)
    return pl.pallas_call(
        share_kernel,
        in_specs=[
            pl.BlockSpec(memory_space=pltpu.SMEM), WHOLE, WHOLE,
            pl.BlockSpec(memory_space=pl.ANY),
        ],
        out_specs=[WHOLE] * (count * parts),
        out_shape=[out] * (count * parts),
        scratch_shapes=[
            pltpu.VMEM((count, 2, BLOCK, keys), jnp.float32),
            pltpu.VMEM((count * BLOCK, keys), jnp.bfloat16),
            pltpu.SemaphoreType.DMA((count,)),
        ],
        compiler_params=pltpu.CompilerParams(vmem_limit_bytes=SHARE_LIMIT),
        cost_estimate=moved(2 * keys * width + count * BLOCK * (8 * keys + 4 * width), 2 * count * BLOCK * keys * width),
        name="shares",
    )(numbers, logs, queue, logits)


def relay_kernel(a_ref, b_ref, upper_ref, lower_ref, a_out, b_out):
    rows = upper_ref.shape[0]
    a_out[:rows, :] = a_ref[:rows, :]
    a_out[rows:, :] = a_ref[rows:, :] + lower_ref[...]
    b_out[:rows, :] = b_ref[:rows, :] + upper_ref[...]
    b_out[rows:, :] = b_ref[rows:, :]


def relayed(a, b, upper, lower):
    return pl.pallas_call(
        relay_kernel,
        in_specs=[WHOLE] * 4,
        out_specs=[WHOLE] * 2,
        out_shape=[jax.ShapeDtypeStruct(a.shape, a.dtype)] * 2,
        compiler_params=pltpu.CompilerParams(vmem_limit_bytes=SMALL_LIMIT),
        cost_estimate=moved(20 * a.size),
        name="relayed",
    )(a, b, upper, lower)


def split_kernel(*refs):
    places, parts, outs = refs[:2], refs[2:8], refs[8:]
    rows = outs[0].shape[0]
    for half in range(2):
        a, b, c = parts[3 * half : 3 * half + 3]
        for i, k in enumerate((0, *ORDER)):
            at = pl.ds(pl.multiple_of((places[half][0] ^ k) * rows, rows), rows)
            outs[4 * half + i][...] = a[at, :] + (b[at, :] + c[at, :])


def split_sums(places, first, second):
    rows, width = first[0].shape
    outs = pl.pallas_call(
        split_kernel,
        in_specs=[pl.BlockSpec(memory_space=pltpu.SMEM)] * 2 + [WHOLE] * 6,
        out_specs=[WHOLE] * 8,
        out_shape=[jax.ShapeDtypeStruct((rows // 4, width), jnp.float32)] * 8,
        compiler_params=pltpu.CompilerParams(vmem_limit_bytes=SMALL_LIMIT),
        cost_estimate=moved(32 * first[0].size),
        name="split_sums",
    )(*places, *first, *second)
    return outs[:4], outs[4:]


def columns_kernel(*refs):
    out = refs[-1]
    rows = refs[0].shape[0]
    for half in range(2):
        a, b, c, d = (ref[...] for ref in refs[4 * half : 4 * half + 4])
        total = (a + b) + (c + d)
        for k in range(out.shape[0]):
            out[k, half * rows : (half + 1) * rows, :] = total[:, k * BLOCK : (k + 1) * BLOCK]


def column_blocks(first, second):
    rows, width = first[0].shape
    return pl.pallas_call(
        columns_kernel,
        in_specs=[WHOLE] * 8,
        out_specs=WHOLE,
        out_shape=jax.ShapeDtypeStruct((width // BLOCK, 2 * rows, BLOCK), jnp.float32),
        compiler_params=pltpu.CompilerParams(vmem_limit_bytes=SMALL_LIMIT),
        cost_estimate=moved(40 * first[0].size),
        name="column_blocks",
    )(*first, *second)


def total_kernel(pieces_ref, out_ref):
    total = pieces_ref[...].sum(0)
    out_ref[...] = jnp.broadcast_to(total[None], out_ref.shape)


def rows_kernel(blocks_ref, first_ref, second_ref):
    rows = first_ref.shape[0]
    for k in range(blocks_ref.shape[0]):
        at = slice(k * BLOCK, (k + 1) * BLOCK)
        first_ref[:, at] = blocks_ref[k, :rows, :]
        second_ref[:, at] = blocks_ref[k, rows:, :]


def stack_kernel(*refs):
    rows = refs[0].shape[0]
    for half, out in enumerate(refs[8:]):
        for k in range(4):
            out[k * rows : (k + 1) * rows, :] = refs[4 * half + k][...]


def stacked(first, second):
    rows, width = first[0].shape
    return pl.pallas_call(
        stack_kernel,
        in_specs=[WHOLE] * 8,
        out_specs=[WHOLE] * 2,
        out_shape=[jax.ShapeDtypeStruct((4 * rows, width), jnp.float32)] * 2,
        compiler_params=pltpu.CompilerParams(vmem_limit_bytes=SMALL_LIMIT),
        cost_estimate=moved(64 * first[0].size),
        name="stacked",
    )(*first, *second)


def halves_kernel(a, b, upper, lower):
    rows = upper.shape[0]
    upper[...] = a[:rows, :]
    lower[...] = b[rows:, :]


def halves(a, b):
    rows, width = a.shape
    return pl.pallas_call(
        halves_kernel,
        in_specs=[WHOLE] * 2,
        out_specs=[WHOLE] * 2,
        out_shape=[jax.ShapeDtypeStruct((rows // 2, width), jnp.float32)] * 2,
        compiler_params=pltpu.CompilerParams(vmem_limit_bytes=SMALL_LIMIT),
        cost_estimate=moved(8 * a.size),
        name="halves",
    )(a, b)


def assemble_kernel(kinds, x_ref, y_ref, *refs):
    out, sem = refs[-2], refs[-1]
    places = (x_ref[0], y_ref[0]), (y_ref[0], x_ref[0])
    copies = []
    for (half, k, start), ref in zip(kinds, refs):
        outer, inner = places[half]
        for j in range(ref.shape[0] // PART):
            at = 4 * BLOCK * half + (outer ^ k) * BLOCK + (inner ^ (0, *ORDER)[start + j]) * PART
            copies.append(
                pltpu.make_async_copy(
                    ref.at[j * PART : (j + 1) * PART, :],
                    out.at[pl.ds(pl.multiple_of(at, PART), PART), :],
                    sem.at[len(copies)],
                )
            )
    for copy in copies:
        copy.start()
    for copy in copies:
        copy.wait()


def assembled(kinds, pieces, earlier, x, y):
    count = sum(piece.shape[0] for piece in pieces) // PART
    kept = [] if earlier is None else [earlier]
    return pl.pallas_call(
        functools.partial(assemble_kernel, kinds),
        in_specs=[pl.BlockSpec(memory_space=pltpu.SMEM)] * 2
        + [WHOLE] * len(pieces)
        + [pl.BlockSpec(memory_space=pl.ANY)] * len(kept),
        out_specs=pl.BlockSpec(memory_space=pl.ANY),
        out_shape=jax.ShapeDtypeStruct((8 * BLOCK, pieces[0].shape[1]), jnp.float32),
        scratch_shapes=[pltpu.SemaphoreType.DMA((count,))],
        input_output_aliases={2 + len(pieces): 0} if kept else {},
        compiler_params=pltpu.CompilerParams(vmem_limit_bytes=SMALL_LIMIT),
        name="assembled",
    )(x, y, *pieces, *kept)


def received(part, axis):
    return {k: exchanged(part, axis, k) for k in reversed(ORDER)}


def local(queries, queue, mentor_logit_grid, positives):
    row_count = queries.shape[0]
    key_count = queue.shape[0]
    x, y = (lax.axis_index(axis).astype(jnp.int32) for axis in (X, Y))
    base = (lax.axis_index(QUEUE) * key_count).astype(jnp.int32).reshape(1)
    positives = positives.reshape(8, BLOCK)
    logits, sent = local_stats(base, queries, queue, mentor_logit_grid, positives, 16)
    pieces = lax.all_to_all(sent, (X, Y), 0, 0)
    sent = pl.pallas_call(
        merge_kernel,
        in_specs=[WHOLE],
        out_specs=WHOLE,
        out_shape=jax.ShapeDtypeStruct((8, 32, BLOCK), jnp.float32),
        compiler_params=pltpu.CompilerParams(vmem_limit_bytes=SMALL_LIMIT),
        name="merge_plane",
    )(pieces)
    pieces = lax.all_to_all(sent, Z, 0, 0)
    logs, divergence = pl.pallas_call(
        logs_kernel,
        in_specs=[WHOLE],
        out_specs=[WHOLE] * 2,
        out_shape=[
            jax.ShapeDtypeStruct((16, BLOCK), jnp.float32),
            jax.ShapeDtypeStruct((1, 1), jnp.float32),
        ],
        compiler_params=pltpu.CompilerParams(vmem_limit_bytes=SMALL_LIMIT),
        name="merge_all",
    )(pieces)

    other = lax.ppermute(divergence, "batch", [(0, 1), (1, 0)])

    def share(partners, parts=1):
        numbers = jnp.stack([n for k in partners for n in (x ^ k, 4 + (y ^ k))])
        return shares(numbers, parts, logs, queue, logits)

    far = share((2,), 2)
    ways = (X, 1), (X, 3), (Y, 1), (Y, 3)
    came = [exchanged(part, *way) for part, way in zip(far, ways)]
    near = share((1, 3))
    blocks = [*relayed(near[0], near[2], *came[:2]), *relayed(near[1], near[3], *came[2:])]
    got = [exchanged(block, *way) for block, way in zip(blocks, ways)]
    own = share((0,))
    places = y.reshape(1), x.reshape(1)
    first, second = split_sums(places, [own[0], *got[:2]], [own[1], *got[2:]])
    first = [first[0]] + [exchanged(p, Y, k) for p, k in zip(first[1:], ORDER)]
    second = [second[0]] + [exchanged(p, X, k) for p, k in zip(second[1:], ORDER)]
    blocks = column_blocks(first, second)
    loss_value = (divergence + other) / (row_count * lax.axis_size("batch"))
    blocks, loss_value = lax.optimization_barrier((blocks, loss_value))
    pieces = lax.all_to_all(blocks, Z, 0, 0)
    total = pl.pallas_call(
        total_kernel,
        in_specs=[WHOLE],
        out_specs=WHOLE,
        out_shape=jax.ShapeDtypeStruct(pieces.shape, jnp.float32),
        compiler_params=pltpu.CompilerParams(vmem_limit_bytes=SMALL_LIMIT),
        name="total",
    )(pieces)
    blocks = lax.all_to_all(total, Z, 0, 0)
    rows, width = blocks.shape[1] // 2, queries.shape[1]
    first, second = pl.pallas_call(
        rows_kernel,
        in_specs=[WHOLE],
        out_specs=[WHOLE] * 2,
        out_shape=[jax.ShapeDtypeStruct((rows, width), jnp.float32)] * 2,
        compiler_params=pltpu.CompilerParams(vmem_limit_bytes=SMALL_LIMIT),
        name="row_blocks",
    )(blocks)
    from_y, from_x = received(first, Y), received(second, X)
    first, second = stacked(
        [first, *(from_y[k] for k in ORDER)], [second, *(from_x[k] for k in ORDER)]
    )
    blocks = [exchanged(first, X, 1), exchanged(first, X, 3)]
    blocks += [exchanged(second, Y, 1), exchanged(second, Y, 3)]
    upper_x, lower_x = halves(blocks[1], blocks[0])
    upper_y, lower_y = halves(blocks[3], blocks[2])
    far = [exchanged(upper_x, X, 1), exchanged(lower_x, X, 3)]
    far += [exchanged(upper_y, Y, 1), exchanged(lower_y, Y, 3)]
    places = x.reshape(1), y.reshape(1)
    kinds = (0, 0, 0), (1, 0, 0), (0, 1, 0), (0, 3, 0), (1, 1, 0), (1, 3, 0)
    query_grad = assembled(kinds, [first, second, *blocks], None, *places)
    kinds = (0, 2, 0), (0, 2, 2), (1, 2, 0), (1, 2, 2)
    query_grad = assembled(kinds, far, query_grad, *places)
    return (query_grad, loss_value.reshape(()))


def solution(mesh):
    finer = Mesh(
        mesh.devices.reshape(mesh.shape["batch"], 4, 4, 8),
        ("batch", X, Y, Z),
    )
    return jax.shard_map(
        local,
        mesh=finer,
        in_specs=(P("batch", None), P(QUEUE, None), P("batch", QUEUE), P("batch")),
        out_specs=(P("batch", None), P()),
        check_vma=False,
    )
```

```python
import functools
import math

import jax
import jax.numpy as jnp
from jax import lax
from jax.experimental import pallas as pl
from jax.experimental.pallas import tpu as pltpu
from jax.sharding import Mesh
from jax.sharding import PartitionSpec as P

X, Y, Z = "queue_0", "queue_1", "queue_2"
QUEUE = (X, Y, Z)

score_factor = 3.0
reward_value = 12.0


def exchanged(part, axis, k):
    n = lax.axis_size(axis)
    return lax.ppermute(part, axis, [(i, i ^ k) for i in range(n)])


SHARE_LIMIT = 49 * 1024 * 1024
SMALL_LIMIT = 8 * 1024 * 1024

BLOCK = 128
PART = 32
TILE = 512
LIMIT = 60 * 1024 * 1024
ORDER = (2, 1, 3)
WHOLE = pl.BlockSpec(memory_space=pltpu.VMEM)


def moved(size, flops=0):
    return pl.CostEstimate(flops=flops, bytes_accessed=size, transcendentals=0)


def as_column(row):
    return jnp.broadcast_to(row, (BLOCK, BLOCK)).T[:, :1]


def teacher_logits(mentor, wanted):
    column = lax.broadcasted_iota(jnp.int32, mentor.shape, 1)
    return mentor.astype(jnp.float32) + jnp.where(column == wanted, reward_value, 0.0)


def stats_kernel(
    base_ref, queries_ref, queue_ref, mentor_ref, positives_ref, logits_ref, sent_ref
):
    step = pl.program_id(0)
    scale = score_factor / math.sqrt(queries_ref.shape[1])
    tile = scale * lax.dot_general(
        queries_ref[...], queue_ref[...], (((1,), (1,)), ((), ())),
        preferred_element_type=jnp.float32,
    )
    logits_ref[0] = tile
    for part in range(TILE // BLOCK):
        at = slice(part * BLOCK, (part + 1) * BLOCK)
        number = step * (TILE // BLOCK) + part
        scores = tile[at, :]
        stud_max = jnp.max(scores, axis=1, keepdims=True)
        stud_sum = jnp.sum(jnp.exp(scores - stud_max), axis=1, keepdims=True)
        wanted = as_column(positives_ref[pl.ds(number, 1), :]) - base_ref[0]
        teacher = teacher_logits(mentor_ref[at, :], wanted)
        logits_ref[1, at, :] = teacher
        teach_max = jnp.max(teacher, axis=1, keepdims=True)
        teach_exp = jnp.exp(teacher - teach_max)
        teach_sum = jnp.sum(teach_exp, axis=1, keepdims=True)
        cross_sum = jnp.sum(teach_exp * (teacher - scores), axis=1, keepdims=True)
        lane = lax.broadcasted_iota(jnp.int32, (BLOCK, BLOCK), 1)
        packed = jnp.zeros((BLOCK, BLOCK), jnp.float32)
        for k, column in enumerate((stud_max, stud_sum, teach_max, teach_sum, cross_sum)):
            packed = jnp.where(lane == k, column, packed)
        rows = packed.T
        stud_max, stud_sum = rows[0:1, :], rows[1:2, :]
        teach_max, teach_sum, cross_sum = rows[2:3, :], rows[3:4, :], rows[4:5, :]
        sent = (stud_max, stud_sum, teach_max + jnp.log(teach_sum), cross_sum / teach_sum)
        for k, row in enumerate(sent):
            sent_ref[:, pl.ds(8 * k + number, 1), :] = jnp.broadcast_to(
                row[None], (sent_ref.shape[0], 1, BLOCK)
            )


def local_stats(base, queries, queue, mentor, positives, copies):
    rows, width = queries.shape
    keys = queue.shape[0]
    return pl.pallas_call(
        stats_kernel,
        grid=(rows // TILE,),
        in_specs=[
            pl.BlockSpec(memory_space=pltpu.SMEM),
            pl.BlockSpec((TILE, width), lambda i: (i, 0)),
            pl.BlockSpec((keys, width), lambda i: (0, 0)),
            pl.BlockSpec((TILE, keys), lambda i: (i, 0)),
            pl.BlockSpec((8, BLOCK), lambda i: (0, 0)),
        ],
        out_specs=[
            pl.BlockSpec((2, TILE, keys), lambda i: (0, i, 0)),
            pl.BlockSpec((copies, 32, BLOCK), lambda i: (0, 0, 0)),
        ],
        out_shape=[
            jax.ShapeDtypeStruct((2, rows, keys), jnp.float32),
            jax.ShapeDtypeStruct((copies, 32, BLOCK), jnp.float32),
        ],
        compiler_params=pltpu.CompilerParams(vmem_limit_bytes=LIMIT),
        name="local_stats",
    )(base, queries, queue, mentor, positives)


def merge(pieces):
    tops, totals, logs, means = (pieces[:, 8 * k : 8 * k + 8] for k in range(4))
    stud_top = tops.max(0)
    stud_total = (totals * jnp.exp(tops - stud_top)).sum(0)
    teach_top = logs.max(0)
    factor = jnp.exp(logs - teach_top)
    total = factor.sum(0)
    return stud_top, stud_total, teach_top + jnp.log(total), (factor * means).sum(0) / total


def merge_kernel(pieces_ref, out_ref):
    for k, value in enumerate(merge(pieces_ref[...])):
        out_ref[:, 8 * k : 8 * k + 8, :] = jnp.broadcast_to(
            value[None], (out_ref.shape[0], 8, BLOCK)
        )


def logs_kernel(pieces_ref, logs_ref, total_ref):
    stud_top, stud_total, teach_log, cross = merge(pieces_ref[...])
    stud_log = stud_top + jnp.log(stud_total)
    logs_ref[0:8, :] = stud_log
    logs_ref[8:16, :] = teach_log
    total = jnp.sum(cross - teach_log + stud_log)
    total_ref[...] = jnp.broadcast_to(total, total_ref.shape)


def share_kernel(numbers_ref, logs_ref, queue_ref, logits_hbm, *refs):
    outs, (logits_ref, weights_ref, sem) = refs[:-3], refs[-3:]
    copies = []
    for k in range(numbers_ref.shape[0]):
        at = pl.ds(pl.multiple_of(numbers_ref[k] * BLOCK, BLOCK), BLOCK)
        copies.append(
            pltpu.make_async_copy(logits_hbm.at[:, at, :], logits_ref.at[k], sem.at[k])
        )
        copies[k].start()
    for k, copy in enumerate(copies):
        number = numbers_ref[k]
        stud_log = as_column(logs_ref[pl.ds(number, 1), :])
        teach_log = as_column(logs_ref[pl.ds(8 + number, 1), :])
        copy.wait()
        weights = jnp.exp(logits_ref[k, 0] - stud_log) - jnp.exp(logits_ref[k, 1] - teach_log)
        weights_ref[k * BLOCK : (k + 1) * BLOCK, :] = weights.astype(jnp.bfloat16)
    total = jnp.dot(weights_ref[...], queue_ref[...], preferred_element_type=jnp.float32)
    rows = outs[0].shape[0]
    for k, out in enumerate(outs):
        out[...] = total[k * rows : (k + 1) * rows, :]


def shares(numbers, parts, logs, queue, logits):
    count = numbers.shape[0]
    keys, width = queue.shape
    out = jax.ShapeDtypeStruct((BLOCK // parts, width), jnp.float32)
    return pl.pallas_call(
        share_kernel,
        in_specs=[
            pl.BlockSpec(memory_space=pltpu.SMEM), WHOLE, WHOLE,
            pl.BlockSpec(memory_space=pl.ANY),
        ],
        out_specs=[WHOLE] * (count * parts),
        out_shape=[out] * (count * parts),
        scratch_shapes=[
            pltpu.VMEM((count, 2, BLOCK, keys), jnp.float32),
            pltpu.VMEM((count * BLOCK, keys), jnp.bfloat16),
            pltpu.SemaphoreType.DMA((count,)),
        ],
        compiler_params=pltpu.CompilerParams(vmem_limit_bytes=SHARE_LIMIT),
        cost_estimate=moved(2 * keys * width + count * BLOCK * (8 * keys + 4 * width), 2 * count * BLOCK * keys * width),
        name="shares",
    )(numbers, logs, queue, logits)


def relay_kernel(a_ref, b_ref, upper_ref, lower_ref, a_out, b_out):
    rows = upper_ref.shape[0]
    a_out[:rows, :] = a_ref[:rows, :]
    a_out[rows:, :] = a_ref[rows:, :] + lower_ref[...]
    b_out[:rows, :] = b_ref[:rows, :] + upper_ref[...]
    b_out[rows:, :] = b_ref[rows:, :]


def relayed(a, b, upper, lower):
    return pl.pallas_call(
        relay_kernel,
        in_specs=[WHOLE] * 4,
        out_specs=[WHOLE] * 2,
        out_shape=[jax.ShapeDtypeStruct(a.shape, a.dtype)] * 2,
        compiler_params=pltpu.CompilerParams(vmem_limit_bytes=SMALL_LIMIT),
        cost_estimate=moved(20 * a.size),
        name="relayed",
    )(a, b, upper, lower)


def split_kernel(*refs):
    places, parts, outs = refs[:2], refs[2:8], refs[8:]
    rows = outs[0].shape[0]
    for half in range(2):
        a, b, c = parts[3 * half : 3 * half + 3]
        for i, k in enumerate((0, *ORDER)):
            at = pl.ds(pl.multiple_of((places[half][0] ^ k) * rows, rows), rows)
            outs[4 * half + i][...] = a[at, :] + (b[at, :] + c[at, :])


def split_sums(places, first, second):
    rows, width = first[0].shape
    outs = pl.pallas_call(
        split_kernel,
        in_specs=[pl.BlockSpec(memory_space=pltpu.SMEM)] * 2 + [WHOLE] * 6,
        out_specs=[WHOLE] * 8,
        out_shape=[jax.ShapeDtypeStruct((rows // 4, width), jnp.float32)] * 8,
        compiler_params=pltpu.CompilerParams(vmem_limit_bytes=SMALL_LIMIT),
        cost_estimate=moved(32 * first[0].size),
        name="split_sums",
    )(*places, *first, *second)
    return outs[:4], outs[4:]


def columns_kernel(*refs):
    out = refs[-1]
    rows = refs[0].shape[0]
    for half in range(2):
        a, b, c, d = (ref[...] for ref in refs[4 * half : 4 * half + 4])
        total = (a + b) + (c + d)
        for k in range(out.shape[0]):
            out[k, half * rows : (half + 1) * rows, :] = total[:, k * BLOCK : (k + 1) * BLOCK]


def column_blocks(first, second):
    rows, width = first[0].shape
    return pl.pallas_call(
        columns_kernel,
        in_specs=[WHOLE] * 8,
        out_specs=WHOLE,
        out_shape=jax.ShapeDtypeStruct((width // BLOCK, 2 * rows, BLOCK), jnp.float32),
        compiler_params=pltpu.CompilerParams(vmem_limit_bytes=SMALL_LIMIT),
        cost_estimate=moved(40 * first[0].size),
        name="column_blocks",
    )(*first, *second)


def total_kernel(pieces_ref, out_ref):
    total = pieces_ref[...].sum(0)
    out_ref[...] = jnp.broadcast_to(total[None], out_ref.shape)


def rows_kernel(blocks_ref, first_ref, second_ref):
    rows = first_ref.shape[0]
    for k in range(blocks_ref.shape[0]):
        at = slice(k * BLOCK, (k + 1) * BLOCK)
        first_ref[:, at] = blocks_ref[k, :rows, :]
        second_ref[:, at] = blocks_ref[k, rows:, :]


def stack_kernel(*refs):
    rows = refs[0].shape[0]
    for half, out in enumerate(refs[8:]):
        for k in range(4):
            out[k * rows : (k + 1) * rows, :] = refs[4 * half + k][...]


def stacked(first, second):
    rows, width = first[0].shape
    return pl.pallas_call(
        stack_kernel,
        in_specs=[WHOLE] * 8,
        out_specs=[WHOLE] * 2,
        out_shape=[jax.ShapeDtypeStruct((4 * rows, width), jnp.float32)] * 2,
        compiler_params=pltpu.CompilerParams(vmem_limit_bytes=SMALL_LIMIT),
        cost_estimate=moved(64 * first[0].size),
        name="stacked",
    )(*first, *second)


def halves_kernel(a, b, upper, lower):
    rows = upper.shape[0]
    upper[...] = a[:rows, :]
    lower[...] = b[rows:, :]


def halves(a, b):
    rows, width = a.shape
    return pl.pallas_call(
        halves_kernel,
        in_specs=[WHOLE] * 2,
        out_specs=[WHOLE] * 2,
        out_shape=[jax.ShapeDtypeStruct((rows // 2, width), jnp.float32)] * 2,
        compiler_params=pltpu.CompilerParams(vmem_limit_bytes=SMALL_LIMIT),
        cost_estimate=moved(8 * a.size),
        name="halves",
    )(a, b)


def assemble_kernel(kinds, x_ref, y_ref, *refs):
    out, sem = refs[-2], refs[-1]
    places = (x_ref[0], y_ref[0]), (y_ref[0], x_ref[0])
    copies = []
    for (half, k, start), ref in zip(kinds, refs):
        outer, inner = places[half]
        for j in range(ref.shape[0] // PART):
            at = 4 * BLOCK * half + (outer ^ k) * BLOCK + (inner ^ (0, *ORDER)[start + j]) * PART
            copies.append(
                pltpu.make_async_copy(
                    ref.at[j * PART : (j + 1) * PART, :],
                    out.at[pl.ds(pl.multiple_of(at, PART), PART), :],
                    sem.at[len(copies)],
                )
            )
    for copy in copies:
        copy.start()
    for copy in copies:
        copy.wait()


def assembled(kinds, pieces, earlier, x, y):
    count = sum(piece.shape[0] for piece in pieces) // PART
    kept = [] if earlier is None else [earlier]
    return pl.pallas_call(
        functools.partial(assemble_kernel, kinds),
        in_specs=[pl.BlockSpec(memory_space=pltpu.SMEM)] * 2
        + [WHOLE] * len(pieces)
        + [pl.BlockSpec(memory_space=pl.ANY)] * len(kept),
        out_specs=pl.BlockSpec(memory_space=pl.ANY),
        out_shape=jax.ShapeDtypeStruct((8 * BLOCK, pieces[0].shape[1]), jnp.float32),
        scratch_shapes=[pltpu.SemaphoreType.DMA((count,))],
        input_output_aliases={2 + len(pieces): 0} if kept else {},
        compiler_params=pltpu.CompilerParams(vmem_limit_bytes=SMALL_LIMIT),
        name="assembled",
    )(x, y, *pieces, *kept)


def received(part, axis):
    return {k: exchanged(part, axis, k) for k in reversed(ORDER)}


def local(queries, queue, mentor_logit_grid, positives):
    row_count = queries.shape[0]
    key_count = queue.shape[0]
    x, y = (lax.axis_index(axis).astype(jnp.int32) for axis in (X, Y))
    base = (lax.axis_index(QUEUE) * key_count).astype(jnp.int32).reshape(1)
    positives = positives.reshape(8, BLOCK)
    logits, sent = local_stats(base, queries, queue, mentor_logit_grid, positives, 16)
    pieces = lax.all_to_all(sent, (X, Y), 0, 0)
    sent = pl.pallas_call(
        merge_kernel,
        in_specs=[WHOLE],
        out_specs=WHOLE,
        out_shape=jax.ShapeDtypeStruct((8, 32, BLOCK), jnp.float32),
        compiler_params=pltpu.CompilerParams(vmem_limit_bytes=SMALL_LIMIT),
        name="merge_plane",
    )(pieces)
    pieces = lax.all_to_all(sent, Z, 0, 0)
    logs, divergence = pl.pallas_call(
        logs_kernel,
        in_specs=[WHOLE],
        out_specs=[WHOLE] * 2,
        out_shape=[
            jax.ShapeDtypeStruct((16, BLOCK), jnp.float32),
            jax.ShapeDtypeStruct((1, 1), jnp.float32),
        ],
        compiler_params=pltpu.CompilerParams(vmem_limit_bytes=SMALL_LIMIT),
        name="merge_all",
    )(pieces)

    other = lax.ppermute(divergence, "batch", [(0, 1), (1, 0)])

    def share(partners, parts=1):
        numbers = jnp.stack([n for k in partners for n in (x ^ k, 4 + (y ^ k))])
        return shares(numbers, parts, logs, queue, logits)

    far = share((2,), 2)
    ways = (X, 1), (X, 3), (Y, 1), (Y, 3)
    came = [exchanged(part, *way) for part, way in zip(far, ways)]
    near = share((1, 3))
    blocks = [*relayed(near[0], near[2], *came[:2]), *relayed(near[1], near[3], *came[2:])]
    got = [exchanged(block, *way) for block, way in zip(blocks, ways)]
    own = share((0,))
    loss_value = (divergence + other) / (row_count * lax.axis_size("batch"))
    own, loss_value = lax.optimization_barrier((own, loss_value))
    places = y.reshape(1), x.reshape(1)
    first, second = split_sums(places, [own[0], *got[:2]], [own[1], *got[2:]])
    first = [first[0]] + [exchanged(p, Y, k) for p, k in zip(first[1:], ORDER)]
    second = [second[0]] + [exchanged(p, X, k) for p, k in zip(second[1:], ORDER)]
    blocks = column_blocks(first, second)
    pieces = lax.all_to_all(blocks, Z, 0, 0)
    total = pl.pallas_call(
        total_kernel,
        in_specs=[WHOLE],
        out_specs=WHOLE,
        out_shape=jax.ShapeDtypeStruct(pieces.shape, jnp.float32),
        compiler_params=pltpu.CompilerParams(vmem_limit_bytes=SMALL_LIMIT),
        name="total",
    )(pieces)
    blocks = lax.all_to_all(total, Z, 0, 0)
    rows, width = blocks.shape[1] // 2, queries.shape[1]
    first, second = pl.pallas_call(
        rows_kernel,
        in_specs=[WHOLE],
        out_specs=[WHOLE] * 2,
        out_shape=[jax.ShapeDtypeStruct((rows, width), jnp.float32)] * 2,
        compiler_params=pltpu.CompilerParams(vmem_limit_bytes=SMALL_LIMIT),
        name="row_blocks",
    )(blocks)
    from_y, from_x = received(first, Y), received(second, X)
    first, second = stacked(
        [first, *(from_y[k] for k in ORDER)], [second, *(from_x[k] for k in ORDER)]
    )
    blocks = [exchanged(first, X, 1), exchanged(first, X, 3)]
    blocks += [exchanged(second, Y, 1), exchanged(second, Y, 3)]
    upper_x, lower_x = halves(blocks[1], blocks[0])
    upper_y, lower_y = halves(blocks[3], blocks[2])
    far = [exchanged(upper_x, X, 1), exchanged(lower_x, X, 3)]
    far += [exchanged(upper_y, Y, 1), exchanged(lower_y, Y, 3)]
    places = x.reshape(1), y.reshape(1)
    kinds = (0, 0, 0), (1, 0, 0), (0, 1, 0), (0, 3, 0), (1, 1, 0), (1, 3, 0)
    query_grad = assembled(kinds, [first, second, *blocks], None, *places)
    kinds = (0, 2, 0), (0, 2, 2), (1, 2, 0), (1, 2, 2)
    query_grad = assembled(kinds, far, query_grad, *places)
    return (query_grad, loss_value.reshape(()))


def solution(mesh):
    finer = Mesh(
        mesh.devices.reshape(mesh.shape["batch"], 4, 4, 8),
        ("batch", X, Y, Z),
    )
    return jax.shard_map(
        local,
        mesh=finer,
        in_specs=(P("batch", None), P(QUEUE, None), P("batch", QUEUE), P("batch")),
        out_specs=(P("batch", None), P()),
        check_vma=False,
    )
```

```python
import functools
import math

import jax
import jax.numpy as jnp
from jax import lax
from jax.experimental import pallas as pl
from jax.experimental.pallas import tpu as pltpu
from jax.sharding import Mesh
from jax.sharding import PartitionSpec as P

X, Y, Z = "queue_0", "queue_1", "queue_2"
QUEUE = (X, Y, Z)

score_factor = 3.0
reward_value = 12.0


def exchanged(part, axis, k):
    n = lax.axis_size(axis)
    return lax.ppermute(part, axis, [(i, i ^ k) for i in range(n)])


SHARE_LIMIT = 44 * 1024 * 1024
SMALL_LIMIT = 8 * 1024 * 1024

BLOCK = 128
PART = 32
TILE = 512
LIMIT = 60 * 1024 * 1024
ORDER = (2, 1, 3)
WHOLE = pl.BlockSpec(memory_space=pltpu.VMEM)


def moved(size, flops=0):
    return pl.CostEstimate(flops=flops, bytes_accessed=size, transcendentals=0)


def as_column(row):
    return jnp.broadcast_to(row, (BLOCK, BLOCK)).T[:, :1]


def teacher_logits(mentor, wanted):
    column = lax.broadcasted_iota(jnp.int32, mentor.shape, 1)
    return mentor.astype(jnp.float32) + jnp.where(column == wanted, reward_value, 0.0)


def stats_kernel(
    base_ref, queries_ref, queue_ref, mentor_ref, positives_ref, scores_ref, kept_ref, sent_ref
):
    step = pl.program_id(0)
    scale = score_factor / math.sqrt(queries_ref.shape[1])
    tile = scale * lax.dot_general(
        queries_ref[...], queue_ref[...], (((1,), (1,)), ((), ())),
        preferred_element_type=jnp.float32,
    )
    scores_ref[0] = tile
    kept_ref[0] = mentor_ref[...]
    for part in range(TILE // BLOCK):
        at = slice(part * BLOCK, (part + 1) * BLOCK)
        number = step * (TILE // BLOCK) + part
        scores = tile[at, :]
        stud_max = jnp.max(scores, axis=1, keepdims=True)
        stud_sum = jnp.sum(jnp.exp(scores - stud_max), axis=1, keepdims=True)
        wanted = as_column(positives_ref[pl.ds(number, 1), :]) - base_ref[0]
        teacher = teacher_logits(mentor_ref[at, :], wanted)
        teach_max = jnp.max(teacher, axis=1, keepdims=True)
        teach_exp = jnp.exp(teacher - teach_max)
        teach_sum = jnp.sum(teach_exp, axis=1, keepdims=True)
        cross_sum = jnp.sum(teach_exp * (teacher - scores), axis=1, keepdims=True)
        lane = lax.broadcasted_iota(jnp.int32, (BLOCK, BLOCK), 1)
        packed = jnp.zeros((BLOCK, BLOCK), jnp.float32)
        for k, column in enumerate((stud_max, stud_sum, teach_max, teach_sum, cross_sum)):
            packed = jnp.where(lane == k, column, packed)
        rows = packed.T
        stud_max, stud_sum = rows[0:1, :], rows[1:2, :]
        teach_max, teach_sum, cross_sum = rows[2:3, :], rows[3:4, :], rows[4:5, :]
        sent = (stud_max, stud_sum, teach_max + jnp.log(teach_sum), cross_sum / teach_sum)
        for k, row in enumerate(sent):
            sent_ref[:, pl.ds(8 * k + number, 1), :] = jnp.broadcast_to(
                row[None], (sent_ref.shape[0], 1, BLOCK)
            )


def local_stats(base, queries, queue, mentor, positives, copies):
    rows, width = queries.shape
    keys = queue.shape[0]
    return pl.pallas_call(
        stats_kernel,
        grid=(rows // TILE,),
        in_specs=[
            pl.BlockSpec(memory_space=pltpu.SMEM),
            pl.BlockSpec((TILE, width), lambda i: (i, 0)),
            pl.BlockSpec((keys, width), lambda i: (0, 0)),
            pl.BlockSpec((TILE, keys), lambda i: (i, 0)),
            pl.BlockSpec((8, BLOCK), lambda i: (0, 0)),
        ],
        out_specs=[
            pl.BlockSpec((1, TILE, keys), lambda i: (0, i, 0)),
            pl.BlockSpec((1, TILE, keys), lambda i: (0, i, 0)),
            pl.BlockSpec((copies, 32, BLOCK), lambda i: (0, 0, 0)),
        ],
        out_shape=[
            jax.ShapeDtypeStruct((3, rows, keys), jnp.float32),
            jax.ShapeDtypeStruct((6, rows, keys), mentor.dtype),
            jax.ShapeDtypeStruct((copies, 32, BLOCK), jnp.float32),
        ],
        compiler_params=pltpu.CompilerParams(vmem_limit_bytes=LIMIT),
        name="local_stats",
    )(base, queries, queue, mentor, positives)


def merge(pieces):
    tops, totals, logs, means = (pieces[:, 8 * k : 8 * k + 8] for k in range(4))
    stud_top = tops.max(0)
    stud_total = (totals * jnp.exp(tops - stud_top)).sum(0)
    teach_top = logs.max(0)
    factor = jnp.exp(logs - teach_top)
    total = factor.sum(0)
    return stud_top, stud_total, teach_top + jnp.log(total), (factor * means).sum(0) / total


def merge_kernel(pieces_ref, out_ref):
    for k, value in enumerate(merge(pieces_ref[...])):
        out_ref[:, 8 * k : 8 * k + 8, :] = jnp.broadcast_to(
            value[None], (out_ref.shape[0], 8, BLOCK)
        )


def logs_kernel(pieces_ref, logs_ref, total_ref):
    stud_top, stud_total, teach_log, cross = merge(pieces_ref[...])
    stud_log = stud_top + jnp.log(stud_total)
    logs_ref[0:8, :] = stud_log
    logs_ref[8:16, :] = teach_log
    total = jnp.sum(cross - teach_log + stud_log)
    total_ref[...] = jnp.broadcast_to(total, total_ref.shape)


def share_kernel(
    numbers_ref, base_ref, logs_ref, positives_ref, queue_ref, scores_hbm, mentor_hbm, *refs
):
    outs, (scores_ref, mentor_ref, weights_ref, sem) = refs[:-4], refs[-4:]
    copies = []
    for k in range(numbers_ref.shape[0]):
        at = pl.ds(pl.multiple_of(numbers_ref[k] * BLOCK, BLOCK), BLOCK)
        copies.append(
            [
                pltpu.make_async_copy(mentor_hbm.at[0, at, :], mentor_ref.at[k], sem.at[2 * k]),
                pltpu.make_async_copy(scores_hbm.at[0, at, :], scores_ref.at[k], sem.at[2 * k + 1]),
            ]
        )
        for copy in copies[k]:
            copy.start()

    def weigh(k):
        number = numbers_ref[k]
        stud_log = as_column(logs_ref[pl.ds(number, 1), :])
        teach_log = as_column(logs_ref[pl.ds(8 + number, 1), :])
        wanted = as_column(positives_ref[pl.ds(number, 1), :]) - base_ref[0]
        for copy in copies[k]:
            copy.wait()
        weights = jnp.exp(scores_ref[k] - stud_log) - jnp.exp(
            teacher_logits(mentor_ref[k], wanted) - teach_log
        )
        weights_ref[k * BLOCK : (k + 1) * BLOCK, :] = weights.astype(jnp.bfloat16)

    rows = outs[0].shape[0]
    for first in range(0, len(copies), 2):
        for k in (first, first + 1):
            weigh(k)
        total = jnp.dot(
            weights_ref[first * BLOCK : (first + 2) * BLOCK, :], queue_ref[...],
            preferred_element_type=jnp.float32,
        )
        each = 2 * BLOCK // rows
        for k in range(each):
            outs[first // 2 * each + k][...] = total[k * rows : (k + 1) * rows, :]


def shares(numbers, parts, base, logs, positives, scores, mentor, queue):
    count = numbers.shape[0]
    keys, width = queue.shape
    out = jax.ShapeDtypeStruct((BLOCK // parts, width), jnp.float32)
    return pl.pallas_call(
        share_kernel,
        in_specs=[pl.BlockSpec(memory_space=pltpu.SMEM)] * 2
        + [WHOLE] * 3
        + [pl.BlockSpec(memory_space=pl.ANY)] * 2,
        out_specs=[WHOLE] * (count * parts),
        out_shape=[out] * (count * parts),
        scratch_shapes=[
            pltpu.VMEM((count, BLOCK, keys), jnp.float32),
            pltpu.VMEM((count, BLOCK, keys), jnp.bfloat16),
            pltpu.VMEM((count * BLOCK, keys), jnp.bfloat16),
            pltpu.SemaphoreType.DMA((2 * count,)),
        ],
        compiler_params=pltpu.CompilerParams(vmem_limit_bytes=SHARE_LIMIT),
        cost_estimate=moved(
            2 * keys * width + count * BLOCK * (6 * keys + 4 * width),
            2 * count * BLOCK * keys * width,
        ),
        name="shares",
    )(numbers, base, logs, positives, queue, scores, mentor)


def relay_kernel(a_ref, b_ref, upper_ref, lower_ref, a_out, b_out):
    rows = upper_ref.shape[0]
    a_out[:rows, :] = a_ref[:rows, :]
    a_out[rows:, :] = a_ref[rows:, :] + lower_ref[...]
    b_out[:rows, :] = b_ref[:rows, :] + upper_ref[...]
    b_out[rows:, :] = b_ref[rows:, :]


def relayed(a, b, upper, lower):
    return pl.pallas_call(
        relay_kernel,
        in_specs=[WHOLE] * 4,
        out_specs=[WHOLE] * 2,
        out_shape=[jax.ShapeDtypeStruct(a.shape, a.dtype)] * 2,
        compiler_params=pltpu.CompilerParams(vmem_limit_bytes=SMALL_LIMIT),
        cost_estimate=moved(20 * a.size),
        name="relayed",
    )(a, b, upper, lower)


def split_kernel(*refs):
    places, parts, outs = refs[:2], refs[2:8], refs[8:]
    rows = outs[0].shape[0]
    for half in range(2):
        a, b, c = parts[3 * half : 3 * half + 3]
        for i, k in enumerate((0, *ORDER)):
            at = pl.ds(pl.multiple_of((places[half][0] ^ k) * rows, rows), rows)
            outs[4 * half + i][...] = a[at, :] + (b[at, :] + c[at, :])


def split_sums(places, first, second):
    rows, width = first[0].shape
    outs = pl.pallas_call(
        split_kernel,
        in_specs=[pl.BlockSpec(memory_space=pltpu.SMEM)] * 2 + [WHOLE] * 6,
        out_specs=[WHOLE] * 8,
        out_shape=[jax.ShapeDtypeStruct((rows // 4, width), jnp.float32)] * 8,
        compiler_params=pltpu.CompilerParams(vmem_limit_bytes=SMALL_LIMIT),
        cost_estimate=moved(32 * first[0].size),
        name="split_sums",
    )(*places, *first, *second)
    return outs[:4], outs[4:]


def columns_kernel(*refs):
    out = refs[-1]
    rows = refs[0].shape[0]
    for half in range(2):
        a, b, c, d = (ref[...] for ref in refs[4 * half : 4 * half + 4])
        total = (a + b) + (c + d)
        for k in range(out.shape[0]):
            out[k, half * rows : (half + 1) * rows, :] = total[:, k * BLOCK : (k + 1) * BLOCK]


def column_blocks(first, second):
    rows, width = first[0].shape
    return pl.pallas_call(
        columns_kernel,
        in_specs=[WHOLE] * 8,
        out_specs=WHOLE,
        out_shape=jax.ShapeDtypeStruct((width // BLOCK, 2 * rows, BLOCK), jnp.float32),
        compiler_params=pltpu.CompilerParams(vmem_limit_bytes=SMALL_LIMIT),
        cost_estimate=moved(40 * first[0].size),
        name="column_blocks",
    )(*first, *second)


def total_kernel(pieces_ref, out_ref):
    total = pieces_ref[...].sum(0)
    out_ref[...] = jnp.broadcast_to(total[None], out_ref.shape)


def rows_kernel(blocks_ref, first_ref, second_ref):
    rows = first_ref.shape[0]
    for k in range(blocks_ref.shape[0]):
        at = slice(k * BLOCK, (k + 1) * BLOCK)
        first_ref[:, at] = blocks_ref[k, :rows, :]
        second_ref[:, at] = blocks_ref[k, rows:, :]


def stack_kernel(*refs):
    rows = refs[0].shape[0]
    for half, out in enumerate(refs[8:]):
        for k in range(4):
            out[k * rows : (k + 1) * rows, :] = refs[4 * half + k][...]


def stacked(first, second):
    rows, width = first[0].shape
    return pl.pallas_call(
        stack_kernel,
        in_specs=[WHOLE] * 8,
        out_specs=[WHOLE] * 2,
        out_shape=[jax.ShapeDtypeStruct((4 * rows, width), jnp.float32)] * 2,
        compiler_params=pltpu.CompilerParams(vmem_limit_bytes=SMALL_LIMIT),
        cost_estimate=moved(64 * first[0].size),
        name="stacked",
    )(*first, *second)


def halves_kernel(a, b, upper, lower):
    rows = upper.shape[0]
    upper[...] = a[:rows, :]
    lower[...] = b[rows:, :]


def halves(a, b):
    rows, width = a.shape
    return pl.pallas_call(
        halves_kernel,
        in_specs=[WHOLE] * 2,
        out_specs=[WHOLE] * 2,
        out_shape=[jax.ShapeDtypeStruct((rows // 2, width), jnp.float32)] * 2,
        compiler_params=pltpu.CompilerParams(vmem_limit_bytes=SMALL_LIMIT),
        cost_estimate=moved(8 * a.size),
        name="halves",
    )(a, b)


def assemble_kernel(kinds, x_ref, y_ref, *refs):
    out, sem = refs[-2], refs[-1]
    places = (x_ref[0], y_ref[0]), (y_ref[0], x_ref[0])
    copies = []
    for (half, k, start), ref in zip(kinds, refs):
        outer, inner = places[half]
        for j in range(ref.shape[0] // PART):
            at = 4 * BLOCK * half + (outer ^ k) * BLOCK + (inner ^ (0, *ORDER)[start + j]) * PART
            copies.append(
                pltpu.make_async_copy(
                    ref.at[j * PART : (j + 1) * PART, :],
                    out.at[pl.ds(pl.multiple_of(at, PART), PART), :],
                    sem.at[len(copies)],
                )
            )
    for copy in copies:
        copy.start()
    for copy in copies:
        copy.wait()


def assembled(kinds, pieces, earlier, x, y):
    count = sum(piece.shape[0] for piece in pieces) // PART
    kept = [] if earlier is None else [earlier]
    return pl.pallas_call(
        functools.partial(assemble_kernel, kinds),
        in_specs=[pl.BlockSpec(memory_space=pltpu.SMEM)] * 2
        + [WHOLE] * len(pieces)
        + [pl.BlockSpec(memory_space=pl.ANY)] * len(kept),
        out_specs=pl.BlockSpec(memory_space=pl.ANY),
        out_shape=jax.ShapeDtypeStruct((8 * BLOCK, pieces[0].shape[1]), jnp.float32),
        scratch_shapes=[pltpu.SemaphoreType.DMA((count,))],
        input_output_aliases={2 + len(pieces): 0} if kept else {},
        compiler_params=pltpu.CompilerParams(vmem_limit_bytes=SMALL_LIMIT),
        name="assembled",
    )(x, y, *pieces, *kept)


def received(part, axis):
    return {k: exchanged(part, axis, k) for k in reversed(ORDER)}


def local(queries, queue, mentor_logit_grid, positives):
    row_count = queries.shape[0]
    key_count = queue.shape[0]
    x, y = (lax.axis_index(axis).astype(jnp.int32) for axis in (X, Y))
    base = (lax.axis_index(QUEUE) * key_count).astype(jnp.int32).reshape(1)
    positives = positives.reshape(8, BLOCK)
    scores, mentor, sent = local_stats(base, queries, queue, mentor_logit_grid, positives, 16)
    pieces = lax.all_to_all(sent, (X, Y), 0, 0)
    sent = pl.pallas_call(
        merge_kernel,
        in_specs=[WHOLE],
        out_specs=WHOLE,
        out_shape=jax.ShapeDtypeStruct((8, 32, BLOCK), jnp.float32),
        compiler_params=pltpu.CompilerParams(vmem_limit_bytes=SMALL_LIMIT),
        name="merge_plane",
    )(pieces)
    pieces = lax.all_to_all(sent, Z, 0, 0)
    logs, divergence = pl.pallas_call(
        logs_kernel,
        in_specs=[WHOLE],
        out_specs=[WHOLE] * 2,
        out_shape=[
            jax.ShapeDtypeStruct((16, BLOCK), jnp.float32),
            jax.ShapeDtypeStruct((1, 1), jnp.float32),
        ],
        compiler_params=pltpu.CompilerParams(vmem_limit_bytes=SMALL_LIMIT),
        name="merge_all",
    )(pieces)

    other = lax.ppermute(divergence, "batch", [(0, 1), (1, 0)])

    def share(partners, parts=1):
        numbers = jnp.stack([n for k in partners for n in (x ^ k, 4 + (y ^ k))])
        return shares(numbers, parts, base, logs, positives, scores, mentor, queue)

    far = share((2,), 2)
    ways = (X, 1), (X, 3), (Y, 1), (Y, 3)
    came = [exchanged(part, *way) for part, way in zip(far, ways)]
    near = share((1, 3))
    blocks = [*relayed(near[0], near[2], *came[:2]), *relayed(near[1], near[3], *came[2:])]
    got = [exchanged(block, *way) for block, way in zip(blocks, ways)]
    own = share((0,))
    loss_value = (divergence + other) / (row_count * lax.axis_size("batch"))
    own, loss_value = lax.optimization_barrier((own, loss_value))
    places = y.reshape(1), x.reshape(1)
    first, second = split_sums(places, [own[0], *got[:2]], [own[1], *got[2:]])
    first = [first[0]] + [exchanged(p, Y, k) for p, k in zip(first[1:], ORDER)]
    second = [second[0]] + [exchanged(p, X, k) for p, k in zip(second[1:], ORDER)]
    blocks = column_blocks(first, second)
    pieces = lax.all_to_all(blocks, Z, 0, 0)
    total = pl.pallas_call(
        total_kernel,
        in_specs=[WHOLE],
        out_specs=WHOLE,
        out_shape=jax.ShapeDtypeStruct(pieces.shape, jnp.float32),
        compiler_params=pltpu.CompilerParams(vmem_limit_bytes=SMALL_LIMIT),
        name="total",
    )(pieces)
    blocks = lax.all_to_all(total, Z, 0, 0)
    rows, width = blocks.shape[1] // 2, queries.shape[1]
    first, second = pl.pallas_call(
        rows_kernel,
        in_specs=[WHOLE],
        out_specs=[WHOLE] * 2,
        out_shape=[jax.ShapeDtypeStruct((rows, width), jnp.float32)] * 2,
        compiler_params=pltpu.CompilerParams(vmem_limit_bytes=SMALL_LIMIT),
        name="row_blocks",
    )(blocks)
    from_y, from_x = received(first, Y), received(second, X)
    first, second = stacked(
        [first, *(from_y[k] for k in ORDER)], [second, *(from_x[k] for k in ORDER)]
    )
    blocks = [exchanged(first, X, 1), exchanged(first, X, 3)]
    blocks += [exchanged(second, Y, 1), exchanged(second, Y, 3)]
    upper_x, lower_x = halves(blocks[1], blocks[0])
    upper_y, lower_y = halves(blocks[3], blocks[2])
    far = [exchanged(upper_x, X, 1), exchanged(lower_x, X, 3)]
    far += [exchanged(upper_y, Y, 1), exchanged(lower_y, Y, 3)]
    places = x.reshape(1), y.reshape(1)
    kinds = (0, 0, 0), (1, 0, 0), (0, 1, 0), (0, 3, 0), (1, 1, 0), (1, 3, 0)
    query_grad = assembled(kinds, [first, second, *blocks], None, *places)
    kinds = (0, 2, 0), (0, 2, 2), (1, 2, 0), (1, 2, 2)
    query_grad = assembled(kinds, far, query_grad, *places)
    return (query_grad, loss_value.reshape(()))


def solution(mesh):
    finer = Mesh(
        mesh.devices.reshape(mesh.shape["batch"], 4, 4, 8),
        ("batch", X, Y, Z),
    )
    return jax.shard_map(
        local,
        mesh=finer,
        in_specs=(P("batch", None), P(QUEUE, None), P("batch", QUEUE), P("batch")),
        out_specs=(P("batch", None), P()),
        check_vma=False,
    )
```

```python
import functools
import math

import jax
import jax.numpy as jnp
from jax import lax
from jax.experimental import pallas as pl
from jax.experimental.pallas import tpu as pltpu
from jax.sharding import Mesh
from jax.sharding import PartitionSpec as P

X, Y, Z = "queue_0", "queue_1", "queue_2"
QUEUE = (X, Y, Z)

score_factor = 3.0
reward_value = 12.0


def exchanged(part, axis, k):
    n = lax.axis_size(axis)
    return lax.ppermute(part, axis, [(i, i ^ k) for i in range(n)])


SHARE_LIMIT = 44 * 1024 * 1024
SMALL_LIMIT = 8 * 1024 * 1024

BLOCK = 128
PART = 32
TILE = 512
LIMIT = 60 * 1024 * 1024
ORDER = (2, 1, 3)
WHOLE = pl.BlockSpec(memory_space=pltpu.VMEM)


def moved(size, flops=0):
    return pl.CostEstimate(flops=flops, bytes_accessed=size, transcendentals=0)


def as_column(row):
    return jnp.broadcast_to(row, (BLOCK, BLOCK)).T[:, :1]


def teacher_logits(mentor, wanted):
    column = lax.broadcasted_iota(jnp.int32, mentor.shape, 1)
    return mentor.astype(jnp.float32) + jnp.where(column == wanted, reward_value, 0.0)


def stats_kernel(
    base_ref, queries_ref, queue_ref, mentor_ref, positives_ref, scores_ref, kept_ref, sent_ref
):
    step = pl.program_id(0)
    scale = score_factor / math.sqrt(queries_ref.shape[1])
    tile = scale * lax.dot_general(
        queries_ref[...], queue_ref[...], (((1,), (1,)), ((), ())),
        preferred_element_type=jnp.float32,
    )
    scores_ref[0] = tile
    kept_ref[0] = mentor_ref[...]
    for part in range(TILE // BLOCK):
        at = slice(part * BLOCK, (part + 1) * BLOCK)
        number = step * (TILE // BLOCK) + part
        scores = tile[at, :]
        stud_max = jnp.max(scores, axis=1, keepdims=True)
        stud_sum = jnp.sum(jnp.exp(scores - stud_max), axis=1, keepdims=True)
        wanted = as_column(positives_ref[pl.ds(number, 1), :]) - base_ref[0]
        teacher = teacher_logits(mentor_ref[at, :], wanted)
        teach_max = jnp.max(teacher, axis=1, keepdims=True)
        teach_exp = jnp.exp(teacher - teach_max)
        teach_sum = jnp.sum(teach_exp, axis=1, keepdims=True)
        cross_sum = jnp.sum(teach_exp * (teacher - scores), axis=1, keepdims=True)
        lane = lax.broadcasted_iota(jnp.int32, (BLOCK, BLOCK), 1)
        packed = jnp.zeros((BLOCK, BLOCK), jnp.float32)
        for k, column in enumerate((stud_max, stud_sum, teach_max, teach_sum, cross_sum)):
            packed = jnp.where(lane == k, column, packed)
        rows = packed.T
        stud_max, stud_sum = rows[0:1, :], rows[1:2, :]
        teach_max, teach_sum, cross_sum = rows[2:3, :], rows[3:4, :], rows[4:5, :]
        sent = (stud_max, stud_sum, teach_max + jnp.log(teach_sum), cross_sum / teach_sum)
        for k, row in enumerate(sent):
            sent_ref[:, pl.ds(8 * k + number, 1), :] = jnp.broadcast_to(
                row[None], (sent_ref.shape[0], 1, BLOCK)
            )


def local_stats(base, queries, queue, mentor, positives, copies):
    rows, width = queries.shape
    keys = queue.shape[0]
    return pl.pallas_call(
        stats_kernel,
        grid=(rows // TILE,),
        in_specs=[
            pl.BlockSpec(memory_space=pltpu.SMEM),
            pl.BlockSpec((TILE, width), lambda i: (i, 0)),
            pl.BlockSpec((keys, width), lambda i: (0, 0)),
            pl.BlockSpec((TILE, keys), lambda i: (i, 0)),
            pl.BlockSpec((8, BLOCK), lambda i: (0, 0)),
        ],
        out_specs=[
            pl.BlockSpec((1, TILE, keys), lambda i: (0, i, 0)),
            pl.BlockSpec((1, TILE, keys), lambda i: (0, i, 0)),
            pl.BlockSpec((copies, 32, BLOCK), lambda i: (0, 0, 0)),
        ],
        out_shape=[
            jax.ShapeDtypeStruct((3, rows, keys), jnp.float32),
            jax.ShapeDtypeStruct((6, rows, keys), mentor.dtype),
            jax.ShapeDtypeStruct((copies, 32, BLOCK), jnp.float32),
        ],
        compiler_params=pltpu.CompilerParams(vmem_limit_bytes=LIMIT),
        name="local_stats",
    )(base, queries, queue, mentor, positives)


def merge(pieces):
    tops, totals, logs, means = (pieces[:, 8 * k : 8 * k + 8] for k in range(4))
    stud_top = tops.max(0)
    stud_total = (totals * jnp.exp(tops - stud_top)).sum(0)
    teach_top = logs.max(0)
    factor = jnp.exp(logs - teach_top)
    total = factor.sum(0)
    return stud_top, stud_total, teach_top + jnp.log(total), (factor * means).sum(0) / total


def merge_kernel(pieces_ref, out_ref):
    for k, value in enumerate(merge(pieces_ref[...])):
        out_ref[:, 8 * k : 8 * k + 8, :] = jnp.broadcast_to(
            value[None], (out_ref.shape[0], 8, BLOCK)
        )


def logs_kernel(pieces_ref, logs_ref, total_ref):
    stud_top, stud_total, teach_log, cross = merge(pieces_ref[...])
    stud_log = stud_top + jnp.log(stud_total)
    logs_ref[0:8, :] = stud_log
    logs_ref[8:16, :] = teach_log
    total = jnp.sum(cross - teach_log + stud_log)
    total_ref[...] = jnp.broadcast_to(total, total_ref.shape)


def share_kernel(
    numbers_ref, base_ref, logs_ref, positives_ref, queue_ref, scores_hbm, mentor_hbm, *refs
):
    outs, (scores_ref, mentor_ref, weights_ref, sem) = refs[:-4], refs[-4:]
    copies = []
    for k in range(numbers_ref.shape[0]):
        at = pl.ds(pl.multiple_of(numbers_ref[k] * BLOCK, BLOCK), BLOCK)
        copies.append(
            [
                pltpu.make_async_copy(mentor_hbm.at[0, at, :], mentor_ref.at[k], sem.at[2 * k]),
                pltpu.make_async_copy(scores_hbm.at[0, at, :], scores_ref.at[k], sem.at[2 * k + 1]),
            ]
        )
        for copy in copies[k]:
            copy.start()

    def weigh(k):
        number = numbers_ref[k]
        stud_log = as_column(logs_ref[pl.ds(number, 1), :])
        teach_log = as_column(logs_ref[pl.ds(8 + number, 1), :])
        wanted = as_column(positives_ref[pl.ds(number, 1), :]) - base_ref[0]
        for copy in copies[k]:
            copy.wait()
        weights = jnp.exp(scores_ref[k] - stud_log) - jnp.exp(
            teacher_logits(mentor_ref[k], wanted) - teach_log
        )
        weights_ref[k * BLOCK : (k + 1) * BLOCK, :] = weights.astype(jnp.bfloat16)

    rows = outs[0].shape[0]
    for first in range(0, len(copies), 2):
        for k in (first, first + 1):
            weigh(k)
        total = jnp.dot(
            weights_ref[first * BLOCK : (first + 2) * BLOCK, :], queue_ref[...],
            preferred_element_type=jnp.float32,
        )
        each = 2 * BLOCK // rows
        for k in range(each):
            outs[first // 2 * each + k][...] = total[k * rows : (k + 1) * rows, :]


def shares(numbers, parts, base, logs, positives, scores, mentor, queue):
    count = numbers.shape[0]
    keys, width = queue.shape
    out = jax.ShapeDtypeStruct((BLOCK // parts, width), jnp.float32)
    return pl.pallas_call(
        share_kernel,
        in_specs=[pl.BlockSpec(memory_space=pltpu.SMEM)] * 2
        + [WHOLE] * 3
        + [pl.BlockSpec(memory_space=pl.ANY)] * 2,
        out_specs=[WHOLE] * (count * parts),
        out_shape=[out] * (count * parts),
        scratch_shapes=[
            pltpu.VMEM((count, BLOCK, keys), jnp.float32),
            pltpu.VMEM((count, BLOCK, keys), jnp.bfloat16),
            pltpu.VMEM((count * BLOCK, keys), jnp.bfloat16),
            pltpu.SemaphoreType.DMA((2 * count,)),
        ],
        compiler_params=pltpu.CompilerParams(vmem_limit_bytes=SHARE_LIMIT),
        cost_estimate=moved(
            2 * keys * width + count * BLOCK * (6 * keys + 4 * width),
            2 * count * BLOCK * keys * width,
        ),
        name="shares",
    )(numbers, base, logs, positives, queue, scores, mentor)


def relay_kernel(a_ref, b_ref, upper_ref, lower_ref, a_out, b_out):
    rows = upper_ref.shape[0]
    a_out[:rows, :] = a_ref[:rows, :]
    a_out[rows:, :] = a_ref[rows:, :] + lower_ref[...]
    b_out[:rows, :] = b_ref[:rows, :] + upper_ref[...]
    b_out[rows:, :] = b_ref[rows:, :]


def relayed(a, b, upper, lower):
    return pl.pallas_call(
        relay_kernel,
        in_specs=[WHOLE] * 4,
        out_specs=[WHOLE] * 2,
        out_shape=[jax.ShapeDtypeStruct(a.shape, a.dtype)] * 2,
        compiler_params=pltpu.CompilerParams(vmem_limit_bytes=SMALL_LIMIT),
        cost_estimate=moved(20 * a.size),
        name="relayed",
    )(a, b, upper, lower)


def split_kernel(*refs):
    places, parts, outs = refs[:2], refs[2:8], refs[8:]
    rows = outs[0].shape[0]
    for half in range(2):
        a, b, c = parts[3 * half : 3 * half + 3]
        for i, k in enumerate((0, *ORDER)):
            at = pl.ds(pl.multiple_of((places[half][0] ^ k) * rows, rows), rows)
            outs[4 * half + i][...] = a[at, :] + (b[at, :] + c[at, :])


def split_sums(places, first, second):
    rows, width = first[0].shape
    outs = pl.pallas_call(
        split_kernel,
        in_specs=[pl.BlockSpec(memory_space=pltpu.SMEM)] * 2 + [WHOLE] * 6,
        out_specs=[WHOLE] * 8,
        out_shape=[jax.ShapeDtypeStruct((rows // 4, width), jnp.float32)] * 8,
        compiler_params=pltpu.CompilerParams(vmem_limit_bytes=SMALL_LIMIT),
        cost_estimate=moved(32 * first[0].size),
        name="split_sums",
    )(*places, *first, *second)
    return outs[:4], outs[4:]


def columns_kernel(*refs):
    out = refs[-1]
    rows = refs[0].shape[0]
    for half in range(2):
        a, b, c, d = (ref[...] for ref in refs[4 * half : 4 * half + 4])
        total = (a + b) + (c + d)
        for k in range(out.shape[0]):
            out[k, half * rows : (half + 1) * rows, :] = total[:, k * BLOCK : (k + 1) * BLOCK]


def column_blocks(first, second):
    rows, width = first[0].shape
    return pl.pallas_call(
        columns_kernel,
        in_specs=[WHOLE] * 8,
        out_specs=WHOLE,
        out_shape=jax.ShapeDtypeStruct((width // BLOCK, 2 * rows, BLOCK), jnp.float32),
        compiler_params=pltpu.CompilerParams(vmem_limit_bytes=SMALL_LIMIT),
        cost_estimate=moved(40 * first[0].size),
        name="column_blocks",
    )(*first, *second)


def total_kernel(pieces_ref, out_ref):
    total = pieces_ref[...].sum(0)
    out_ref[...] = jnp.broadcast_to(total[None], out_ref.shape)


def rows_kernel(blocks_ref, first_ref, second_ref):
    rows = first_ref.shape[0]
    for k in range(blocks_ref.shape[0]):
        at = slice(k * BLOCK, (k + 1) * BLOCK)
        first_ref[:, at] = blocks_ref[k, :rows, :]
        second_ref[:, at] = blocks_ref[k, rows:, :]


def stack_kernel(*refs):
    rows = refs[0].shape[0]
    for half, out in enumerate(refs[8:]):
        for k in range(4):
            out[k * rows : (k + 1) * rows, :] = refs[4 * half + k][...]


def stacked(first, second):
    rows, width = first[0].shape
    return pl.pallas_call(
        stack_kernel,
        in_specs=[WHOLE] * 8,
        out_specs=[WHOLE] * 2,
        out_shape=[jax.ShapeDtypeStruct((4 * rows, width), jnp.float32)] * 2,
        compiler_params=pltpu.CompilerParams(vmem_limit_bytes=SMALL_LIMIT),
        cost_estimate=moved(64 * first[0].size),
        name="stacked",
    )(*first, *second)


def halves_kernel(a, b, upper, lower):
    rows = upper.shape[0]
    upper[...] = a[:rows, :]
    lower[...] = b[rows:, :]


def halves(a, b):
    rows, width = a.shape
    return pl.pallas_call(
        halves_kernel,
        in_specs=[WHOLE] * 2,
        out_specs=[WHOLE] * 2,
        out_shape=[jax.ShapeDtypeStruct((rows // 2, width), jnp.float32)] * 2,
        compiler_params=pltpu.CompilerParams(vmem_limit_bytes=SMALL_LIMIT),
        cost_estimate=moved(8 * a.size),
        name="halves",
    )(a, b)


def assemble_kernel(kinds, x_ref, y_ref, *refs):
    out, sem = refs[-2], refs[-1]
    places = (x_ref[0], y_ref[0]), (y_ref[0], x_ref[0])
    copies = []
    for (half, k, start), ref in zip(kinds, refs):
        outer, inner = places[half]
        for j in range(ref.shape[0] // PART):
            at = 4 * BLOCK * half + (outer ^ k) * BLOCK + (inner ^ (0, *ORDER)[start + j]) * PART
            copies.append(
                pltpu.make_async_copy(
                    ref.at[j * PART : (j + 1) * PART, :],
                    out.at[pl.ds(pl.multiple_of(at, PART), PART), :],
                    sem.at[len(copies)],
                )
            )
    for copy in copies:
        copy.start()
    for copy in copies:
        copy.wait()


def assembled(kinds, pieces, earlier, x, y):
    count = sum(piece.shape[0] for piece in pieces) // PART
    kept = [] if earlier is None else [earlier]
    return pl.pallas_call(
        functools.partial(assemble_kernel, kinds),
        in_specs=[pl.BlockSpec(memory_space=pltpu.SMEM)] * 2
        + [WHOLE] * len(pieces)
        + [pl.BlockSpec(memory_space=pl.ANY)] * len(kept),
        out_specs=pl.BlockSpec(memory_space=pl.ANY),
        out_shape=jax.ShapeDtypeStruct((8 * BLOCK, pieces[0].shape[1]), jnp.float32),
        scratch_shapes=[pltpu.SemaphoreType.DMA((count,))],
        input_output_aliases={2 + len(pieces): 0} if kept else {},
        compiler_params=pltpu.CompilerParams(vmem_limit_bytes=SMALL_LIMIT),
        name="assembled",
    )(x, y, *pieces, *kept)


def received(part, axis):
    return {k: exchanged(part, axis, k) for k in reversed(ORDER)}


def local(queries, queue, mentor_logit_grid, positives):
    row_count = queries.shape[0]
    key_count = queue.shape[0]
    x, y = (lax.axis_index(axis).astype(jnp.int32) for axis in (X, Y))
    base = (lax.axis_index(QUEUE) * key_count).astype(jnp.int32).reshape(1)
    positives = positives.reshape(8, BLOCK)
    scores, mentor, sent = local_stats(base, queries, queue, mentor_logit_grid, positives, 16)
    pieces = lax.all_to_all(sent, (X, Y), 0, 0)
    sent = pl.pallas_call(
        merge_kernel,
        in_specs=[WHOLE],
        out_specs=WHOLE,
        out_shape=jax.ShapeDtypeStruct((8, 32, BLOCK), jnp.float32),
        compiler_params=pltpu.CompilerParams(vmem_limit_bytes=SMALL_LIMIT),
        name="merge_plane",
    )(pieces)
    pieces = lax.all_to_all(sent, Z, 0, 0)
    logs, divergence = pl.pallas_call(
        logs_kernel,
        in_specs=[WHOLE],
        out_specs=[WHOLE] * 2,
        out_shape=[
            jax.ShapeDtypeStruct((16, BLOCK), jnp.float32),
            jax.ShapeDtypeStruct((1, 1), jnp.float32),
        ],
        compiler_params=pltpu.CompilerParams(vmem_limit_bytes=SMALL_LIMIT),
        name="merge_all",
    )(pieces)

    other = lax.ppermute(divergence, "batch", [(0, 1), (1, 0)])

    def share(partners, parts=1):
        numbers = jnp.stack([n for k in partners for n in (x ^ k, 4 + (y ^ k))])
        return shares(numbers, parts, base, logs, positives, scores, mentor, queue)

    far = share((2,), 2)
    ways = (X, 1), (X, 3), (Y, 1), (Y, 3)
    came = [exchanged(part, *way) for part, way in zip(far, ways)]
    near = share((1, 3))
    blocks = [*relayed(near[0], near[2], *came[:2]), *relayed(near[1], near[3], *came[2:])]
    got = [exchanged(block, *way) for block, way in zip(blocks, ways)]
    own = share((0,))
    loss_value = (divergence + other) / (row_count * lax.axis_size("batch"))
    own, loss_value = lax.optimization_barrier((own, loss_value))
    places = y.reshape(1), x.reshape(1)
    first, second = split_sums(places, [own[0], *got[:2]], [own[1], *got[2:]])
    first = [first[0]] + [exchanged(first[i], Y, ORDER[i - 1]) for i in (2, 1, 3)]
    second = [second[0]] + [exchanged(second[i], X, ORDER[i - 1]) for i in (1, 2, 3)]
    blocks = column_blocks(first, second)
    pieces = lax.all_to_all(blocks, Z, 0, 0)
    total = pl.pallas_call(
        total_kernel,
        in_specs=[WHOLE],
        out_specs=WHOLE,
        out_shape=jax.ShapeDtypeStruct(pieces.shape, jnp.float32),
        compiler_params=pltpu.CompilerParams(vmem_limit_bytes=SMALL_LIMIT),
        name="total",
    )(pieces)
    blocks = lax.all_to_all(total, Z, 0, 0)
    rows, width = blocks.shape[1] // 2, queries.shape[1]
    first, second = pl.pallas_call(
        rows_kernel,
        in_specs=[WHOLE],
        out_specs=[WHOLE] * 2,
        out_shape=[jax.ShapeDtypeStruct((rows, width), jnp.float32)] * 2,
        compiler_params=pltpu.CompilerParams(vmem_limit_bytes=SMALL_LIMIT),
        name="row_blocks",
    )(blocks)
    from_y, from_x = received(first, Y), received(second, X)
    first, second = stacked(
        [first, *(from_y[k] for k in ORDER)], [second, *(from_x[k] for k in ORDER)]
    )
    blocks = [exchanged(first, X, 1), exchanged(first, X, 3)]
    blocks += [exchanged(second, Y, 1), exchanged(second, Y, 3)]
    upper_x, lower_x = halves(blocks[1], blocks[0])
    upper_y, lower_y = halves(blocks[3], blocks[2])
    far = [exchanged(upper_x, X, 1), exchanged(lower_x, X, 3)]
    far += [exchanged(upper_y, Y, 1), exchanged(lower_y, Y, 3)]
    places = x.reshape(1), y.reshape(1)
    kinds = (0, 0, 0), (1, 0, 0), (0, 1, 0), (0, 3, 0), (1, 1, 0), (1, 3, 0)
    query_grad = assembled(kinds, [first, second, *blocks], None, *places)
    kinds = (0, 2, 0), (0, 2, 2), (1, 2, 0), (1, 2, 2)
    query_grad = assembled(kinds, far, query_grad, *places)
    return (query_grad, loss_value.reshape(()))


def solution(mesh):
    finer = Mesh(
        mesh.devices.reshape(mesh.shape["batch"], 4, 4, 8),
        ("batch", X, Y, Z),
    )
    return jax.shard_map(
        local,
        mesh=finer,
        in_specs=(P("batch", None), P(QUEUE, None), P("batch", QUEUE), P("batch")),
        out_specs=(P("batch", None), P()),
        check_vma=False,
    )
```

```python
import functools
import math

import jax
import jax.numpy as jnp
from jax import lax
from jax.experimental import pallas as pl
from jax.experimental.pallas import tpu as pltpu
from jax.sharding import Mesh
from jax.sharding import PartitionSpec as P

X, Y, Z = "queue_0", "queue_1", "queue_2"
QUEUE = (X, Y, Z)

score_factor = 3.0
reward_value = 12.0


def exchanged(part, axis, k):
    n = lax.axis_size(axis)
    return lax.ppermute(part, axis, [(i, i ^ k) for i in range(n)])


SHARE_LIMIT = 44 * 1024 * 1024
SMALL_LIMIT = 8 * 1024 * 1024

BLOCK = 128
PART = 32
TILE = 512
LIMIT = 60 * 1024 * 1024
ORDER = (2, 1, 3)
WHOLE = pl.BlockSpec(memory_space=pltpu.VMEM)


def moved(size, flops=0):
    return pl.CostEstimate(flops=flops, bytes_accessed=size, transcendentals=0)


def as_column(row):
    return jnp.broadcast_to(row, (BLOCK, BLOCK)).T[:, :1]


def teacher_logits(mentor, wanted):
    column = lax.broadcasted_iota(jnp.int32, mentor.shape, 1)
    return mentor.astype(jnp.float32) + jnp.where(column == wanted, reward_value, 0.0)


def stats_kernel(
    base_ref, queries_ref, queue_ref, mentor_ref, positives_ref, scores_ref, kept_ref, sent_ref
):
    step = pl.program_id(0)
    scale = score_factor / math.sqrt(queries_ref.shape[1])
    tile = scale * lax.dot_general(
        queries_ref[...], queue_ref[...], (((1,), (1,)), ((), ())),
        preferred_element_type=jnp.float32,
    )
    scores_ref[0] = tile
    kept_ref[0] = mentor_ref[...]
    for part in range(TILE // BLOCK):
        at = slice(part * BLOCK, (part + 1) * BLOCK)
        number = step * (TILE // BLOCK) + part
        scores = tile[at, :]
        stud_max = jnp.max(scores, axis=1, keepdims=True)
        stud_sum = jnp.sum(jnp.exp(scores - stud_max), axis=1, keepdims=True)
        wanted = as_column(positives_ref[pl.ds(number, 1), :]) - base_ref[0]
        teacher = teacher_logits(mentor_ref[at, :], wanted)
        teach_max = jnp.max(teacher, axis=1, keepdims=True)
        teach_exp = jnp.exp(teacher - teach_max)
        teach_sum = jnp.sum(teach_exp, axis=1, keepdims=True)
        cross_sum = jnp.sum(teach_exp * (teacher - scores), axis=1, keepdims=True)
        lane = lax.broadcasted_iota(jnp.int32, (BLOCK, BLOCK), 1)
        packed = jnp.zeros((BLOCK, BLOCK), jnp.float32)
        for k, column in enumerate((stud_max, stud_sum, teach_max, teach_sum, cross_sum)):
            packed = jnp.where(lane == k, column, packed)
        rows = packed.T
        stud_max, stud_sum = rows[0:1, :], rows[1:2, :]
        teach_max, teach_sum, cross_sum = rows[2:3, :], rows[3:4, :], rows[4:5, :]
        sent = (stud_max, stud_sum, teach_max + jnp.log(teach_sum), cross_sum / teach_sum)
        for k, row in enumerate(sent):
            sent_ref[:, pl.ds(8 * k + number, 1), :] = jnp.broadcast_to(
                row[None], (sent_ref.shape[0], 1, BLOCK)
            )


def local_stats(base, queries, queue, mentor, positives, copies):
    rows, width = queries.shape
    keys = queue.shape[0]
    return pl.pallas_call(
        stats_kernel,
        grid=(rows // TILE,),
        in_specs=[
            pl.BlockSpec(memory_space=pltpu.SMEM),
            pl.BlockSpec((TILE, width), lambda i: (i, 0)),
            pl.BlockSpec((keys, width), lambda i: (0, 0)),
            pl.BlockSpec((TILE, keys), lambda i: (i, 0)),
            pl.BlockSpec((8, BLOCK), lambda i: (0, 0)),
        ],
        out_specs=[
            pl.BlockSpec((1, TILE, keys), lambda i: (0, i, 0)),
            pl.BlockSpec((1, TILE, keys), lambda i: (0, i, 0)),
            pl.BlockSpec((copies, 32, BLOCK), lambda i: (0, 0, 0)),
        ],
        out_shape=[
            jax.ShapeDtypeStruct((3, rows, keys), jnp.float32),
            jax.ShapeDtypeStruct((6, rows, keys), mentor.dtype),
            jax.ShapeDtypeStruct((copies, 32, BLOCK), jnp.float32),
        ],
        compiler_params=pltpu.CompilerParams(vmem_limit_bytes=LIMIT),
        name="local_stats",
    )(base, queries, queue, mentor, positives)


def merge(pieces):
    tops, totals, logs, means = (pieces[:, 8 * k : 8 * k + 8] for k in range(4))
    stud_top = tops.max(0)
    stud_total = (totals * jnp.exp(tops - stud_top)).sum(0)
    teach_top = logs.max(0)
    factor = jnp.exp(logs - teach_top)
    total = factor.sum(0)
    return stud_top, stud_total, teach_top + jnp.log(total), (factor * means).sum(0) / total


def merge_kernel(pieces_ref, out_ref):
    for k, value in enumerate(merge(pieces_ref[...])):
        out_ref[:, 8 * k : 8 * k + 8, :] = jnp.broadcast_to(
            value[None], (out_ref.shape[0], 8, BLOCK)
        )


def logs_kernel(pieces_ref, logs_ref, total_ref):
    stud_top, stud_total, teach_log, cross = merge(pieces_ref[...])
    stud_log = stud_top + jnp.log(stud_total)
    logs_ref[0:8, :] = stud_log
    logs_ref[8:16, :] = teach_log
    total = jnp.sum(cross - teach_log + stud_log)
    total_ref[...] = jnp.broadcast_to(total, total_ref.shape)


def share_kernel(
    numbers_ref, base_ref, logs_ref, positives_ref, queue_ref, scores_hbm, mentor_hbm, *refs
):
    outs, (scores_ref, mentor_ref, weights_ref, sem) = refs[:-4], refs[-4:]
    copies = []
    for k in range(numbers_ref.shape[0]):
        at = pl.ds(pl.multiple_of(numbers_ref[k] * BLOCK, BLOCK), BLOCK)
        copies.append(
            [
                pltpu.make_async_copy(mentor_hbm.at[0, at, :], mentor_ref.at[k], sem.at[2 * k]),
                pltpu.make_async_copy(scores_hbm.at[0, at, :], scores_ref.at[k], sem.at[2 * k + 1]),
            ]
        )
        for copy in copies[k]:
            copy.start()

    def weigh(k):
        number = numbers_ref[k]
        stud_log = as_column(logs_ref[pl.ds(number, 1), :])
        teach_log = as_column(logs_ref[pl.ds(8 + number, 1), :])
        wanted = as_column(positives_ref[pl.ds(number, 1), :]) - base_ref[0]
        for copy in copies[k]:
            copy.wait()
        weights = jnp.exp(scores_ref[k] - stud_log) - jnp.exp(
            teacher_logits(mentor_ref[k], wanted) - teach_log
        )
        weights_ref[k * BLOCK : (k + 1) * BLOCK, :] = weights.astype(jnp.bfloat16)

    rows = outs[0].shape[0]
    for first in range(0, len(copies), 2):
        for k in (first, first + 1):
            weigh(k)
        total = jnp.dot(
            weights_ref[first * BLOCK : (first + 2) * BLOCK, :], queue_ref[...],
            preferred_element_type=jnp.float32,
        )
        each = 2 * BLOCK // rows
        for k in range(each):
            outs[first // 2 * each + k][...] = total[k * rows : (k + 1) * rows, :]


def shares(numbers, parts, base, logs, positives, scores, mentor, queue):
    count = numbers.shape[0]
    keys, width = queue.shape
    out = jax.ShapeDtypeStruct((BLOCK // parts, width), jnp.float32)
    return pl.pallas_call(
        share_kernel,
        in_specs=[pl.BlockSpec(memory_space=pltpu.SMEM)] * 2
        + [WHOLE] * 3
        + [pl.BlockSpec(memory_space=pl.ANY)] * 2,
        out_specs=[WHOLE] * (count * parts),
        out_shape=[out] * (count * parts),
        scratch_shapes=[
            pltpu.VMEM((count, BLOCK, keys), jnp.float32),
            pltpu.VMEM((count, BLOCK, keys), jnp.bfloat16),
            pltpu.VMEM((count * BLOCK, keys), jnp.bfloat16),
            pltpu.SemaphoreType.DMA((2 * count,)),
        ],
        compiler_params=pltpu.CompilerParams(vmem_limit_bytes=SHARE_LIMIT),
        cost_estimate=moved(
            2 * keys * width + count * BLOCK * (6 * keys + 4 * width),
            2 * count * BLOCK * keys * width,
        ),
        name="shares",
    )(numbers, base, logs, positives, queue, scores, mentor)


def relay_kernel(a_ref, b_ref, upper_ref, lower_ref, a_out, b_out):
    rows = upper_ref.shape[0]
    a_out[:rows, :] = a_ref[:rows, :]
    a_out[rows:, :] = a_ref[rows:, :] + lower_ref[...]
    b_out[:rows, :] = b_ref[:rows, :] + upper_ref[...]
    b_out[rows:, :] = b_ref[rows:, :]


def relayed(a, b, upper, lower):
    return pl.pallas_call(
        relay_kernel,
        in_specs=[WHOLE] * 4,
        out_specs=[WHOLE] * 2,
        out_shape=[jax.ShapeDtypeStruct(a.shape, a.dtype)] * 2,
        compiler_params=pltpu.CompilerParams(vmem_limit_bytes=SMALL_LIMIT),
        cost_estimate=moved(20 * a.size),
        name="relayed",
    )(a, b, upper, lower)


def split_kernel(*refs):
    places, parts, outs = refs[:2], refs[2:8], refs[8:]
    rows = outs[0].shape[0]
    for half in range(2):
        a, b, c = parts[3 * half : 3 * half + 3]
        for i, k in enumerate((0, *ORDER)):
            at = pl.ds(pl.multiple_of((places[half][0] ^ k) * rows, rows), rows)
            outs[4 * half + i][...] = a[at, :] + (b[at, :] + c[at, :])


def split_sums(places, first, second):
    rows, width = first[0].shape
    outs = pl.pallas_call(
        split_kernel,
        in_specs=[pl.BlockSpec(memory_space=pltpu.SMEM)] * 2 + [WHOLE] * 6,
        out_specs=[WHOLE] * 8,
        out_shape=[jax.ShapeDtypeStruct((rows // 4, width), jnp.float32)] * 8,
        compiler_params=pltpu.CompilerParams(vmem_limit_bytes=SMALL_LIMIT),
        cost_estimate=moved(32 * first[0].size),
        name="split_sums",
    )(*places, *first, *second)
    return outs[:4], outs[4:]


def columns_kernel(*refs):
    out = refs[-1]
    rows = refs[0].shape[0]
    for half in range(2):
        a, b, c, d = (ref[...] for ref in refs[4 * half : 4 * half + 4])
        total = (a + b) + (c + d)
        for k in range(out.shape[0]):
            out[k, half * rows : (half + 1) * rows, :] = total[:, k * BLOCK : (k + 1) * BLOCK]


def column_blocks(first, second):
    rows, width = first[0].shape
    return pl.pallas_call(
        columns_kernel,
        in_specs=[WHOLE] * 8,
        out_specs=WHOLE,
        out_shape=jax.ShapeDtypeStruct((width // BLOCK, 2 * rows, BLOCK), jnp.float32),
        compiler_params=pltpu.CompilerParams(vmem_limit_bytes=SMALL_LIMIT),
        cost_estimate=moved(40 * first[0].size),
        name="column_blocks",
    )(*first, *second)


def total_kernel(pieces_ref, out_ref):
    total = pieces_ref[...].sum(0)
    out_ref[...] = jnp.broadcast_to(total[None], out_ref.shape)


def rows_kernel(blocks_ref, first_ref, second_ref):
    rows = first_ref.shape[0]
    for k in range(blocks_ref.shape[0]):
        at = slice(k * BLOCK, (k + 1) * BLOCK)
        first_ref[:, at] = blocks_ref[k, :rows, :]
        second_ref[:, at] = blocks_ref[k, rows:, :]


def stack_kernel(*refs):
    rows = refs[0].shape[0]
    for half, out in enumerate(refs[8:]):
        for k in range(4):
            out[k * rows : (k + 1) * rows, :] = refs[4 * half + k][...]


def stacked(first, second):
    rows, width = first[0].shape
    return pl.pallas_call(
        stack_kernel,
        in_specs=[WHOLE] * 8,
        out_specs=[WHOLE] * 2,
        out_shape=[jax.ShapeDtypeStruct((4 * rows, width), jnp.float32)] * 2,
        compiler_params=pltpu.CompilerParams(vmem_limit_bytes=SMALL_LIMIT),
        cost_estimate=moved(64 * first[0].size),
        name="stacked",
    )(*first, *second)


def halves_kernel(a, b, upper, lower):
    rows = upper.shape[0]
    upper[...] = a[:rows, :]
    lower[...] = b[rows:, :]


def halves(a, b):
    rows, width = a.shape
    return pl.pallas_call(
        halves_kernel,
        in_specs=[WHOLE] * 2,
        out_specs=[WHOLE] * 2,
        out_shape=[jax.ShapeDtypeStruct((rows // 2, width), jnp.float32)] * 2,
        compiler_params=pltpu.CompilerParams(vmem_limit_bytes=SMALL_LIMIT),
        cost_estimate=moved(8 * a.size),
        name="halves",
    )(a, b)


def assemble_kernel(kinds, x_ref, y_ref, *refs):
    out, sem = refs[-2], refs[-1]
    places = (x_ref[0], y_ref[0]), (y_ref[0], x_ref[0])
    copies = []
    for (half, k, start), ref in zip(kinds, refs):
        outer, inner = places[half]
        for j in range(ref.shape[0] // PART):
            at = 4 * BLOCK * half + (outer ^ k) * BLOCK + (inner ^ (0, *ORDER)[start + j]) * PART
            copies.append(
                pltpu.make_async_copy(
                    ref.at[j * PART : (j + 1) * PART, :],
                    out.at[pl.ds(pl.multiple_of(at, PART), PART), :],
                    sem.at[len(copies)],
                )
            )
    for copy in copies:
        copy.start()
    for copy in copies:
        copy.wait()


def assembled(kinds, pieces, earlier, x, y):
    count = sum(piece.shape[0] for piece in pieces) // PART
    kept = [] if earlier is None else [earlier]
    return pl.pallas_call(
        functools.partial(assemble_kernel, kinds),
        in_specs=[pl.BlockSpec(memory_space=pltpu.SMEM)] * 2
        + [WHOLE] * len(pieces)
        + [pl.BlockSpec(memory_space=pl.ANY)] * len(kept),
        out_specs=pl.BlockSpec(memory_space=pl.ANY),
        out_shape=jax.ShapeDtypeStruct((8 * BLOCK, pieces[0].shape[1]), jnp.float32),
        scratch_shapes=[pltpu.SemaphoreType.DMA((count,))],
        input_output_aliases={2 + len(pieces): 0} if kept else {},
        compiler_params=pltpu.CompilerParams(vmem_limit_bytes=SMALL_LIMIT),
        name="assembled",
    )(x, y, *pieces, *kept)


def received(part, axis):
    return {k: exchanged(part, axis, k) for k in reversed(ORDER)}


def local(queries, queue, mentor_logit_grid, positives):
    row_count = queries.shape[0]
    key_count = queue.shape[0]
    x, y = (lax.axis_index(axis).astype(jnp.int32) for axis in (X, Y))
    base = (lax.axis_index(QUEUE) * key_count).astype(jnp.int32).reshape(1)
    positives = positives.reshape(8, BLOCK)
    scores, mentor, sent = local_stats(base, queries, queue, mentor_logit_grid, positives, 16)
    pieces = lax.all_to_all(sent, (X, Y), 0, 0)
    sent = pl.pallas_call(
        merge_kernel,
        in_specs=[WHOLE],
        out_specs=WHOLE,
        out_shape=jax.ShapeDtypeStruct((8, 32, BLOCK), jnp.float32),
        compiler_params=pltpu.CompilerParams(vmem_limit_bytes=SMALL_LIMIT),
        name="merge_plane",
    )(pieces)
    pieces = lax.all_to_all(sent, Z, 0, 0)
    logs, divergence = pl.pallas_call(
        logs_kernel,
        in_specs=[WHOLE],
        out_specs=[WHOLE] * 2,
        out_shape=[
            jax.ShapeDtypeStruct((16, BLOCK), jnp.float32),
            jax.ShapeDtypeStruct((1, 1), jnp.float32),
        ],
        compiler_params=pltpu.CompilerParams(vmem_limit_bytes=SMALL_LIMIT),
        name="merge_all",
    )(pieces)

    other = lax.ppermute(divergence, "batch", [(0, 1), (1, 0)])

    def share(partners, parts=1):
        numbers = jnp.stack([n for k in partners for n in (x ^ k, 4 + (y ^ k))])
        return shares(numbers, parts, base, logs, positives, scores, mentor, queue)

    far = share((2,), 2)
    ways = (X, 1), (X, 3), (Y, 1), (Y, 3)
    came = [exchanged(part, *way) for part, way in zip(far, ways)]
    near = share((1, 3))
    blocks = [*relayed(near[0], near[2], *came[:2]), *relayed(near[1], near[3], *came[2:])]
    got = [exchanged(block, *way) for block, way in zip(blocks, ways)]
    own = share((0,))
    loss_value = (divergence + other) / (row_count * lax.axis_size("batch"))
    own, loss_value = lax.optimization_barrier((own, loss_value))
    places = y.reshape(1), x.reshape(1)
    first, second = split_sums(places, [own[0], *got[:2]], [own[1], *got[2:]])
    first = [first[0]] + [exchanged(first[i], Y, ORDER[i - 1]) for i in (2, 1, 3)]
    second = [second[0]] + [exchanged(second[i], X, ORDER[i - 1]) for i in (1, 2, 3)]
    blocks = column_blocks(first, second)
    pieces = lax.all_to_all(blocks, Z, 0, 0)
    total = pl.pallas_call(
        total_kernel,
        in_specs=[WHOLE],
        out_specs=WHOLE,
        out_shape=jax.ShapeDtypeStruct(pieces.shape, jnp.float32),
        compiler_params=pltpu.CompilerParams(vmem_limit_bytes=SMALL_LIMIT),
        name="total",
    )(pieces)
    blocks = lax.all_to_all(total, Z, 0, 0)
    rows, width = blocks.shape[1] // 2, queries.shape[1]
    first, second = pl.pallas_call(
        rows_kernel,
        in_specs=[WHOLE],
        out_specs=[WHOLE] * 2,
        out_shape=[jax.ShapeDtypeStruct((rows, width), jnp.float32)] * 2,
        compiler_params=pltpu.CompilerParams(vmem_limit_bytes=SMALL_LIMIT),
        name="row_blocks",
    )(blocks)
    from_y, from_x = received(first, Y), received(second, X)
    first, second = stacked(
        [first, *(from_y[k] for k in ORDER)], [second, *(from_x[k] for k in ORDER)]
    )
    blocks = [exchanged(first, X, 1), exchanged(first, X, 3)]
    blocks += [exchanged(second, Y, 1), exchanged(second, Y, 3)]
    upper_x, lower_x = halves(blocks[1], blocks[0])
    upper_y, lower_y = halves(blocks[3], blocks[2])
    far = [exchanged(upper_x, X, 1), exchanged(lower_x, X, 3)]
    far += [exchanged(upper_y, Y, 1), exchanged(lower_y, Y, 3)]
    places = x.reshape(1), y.reshape(1)
    kinds = (0, 0, 0), (1, 0, 0), (0, 1, 0), (0, 3, 0), (1, 1, 0), (1, 3, 0)
    query_grad = assembled(kinds, [first, second, *blocks], None, *places)
    query_grad = assembled(((1, 2, 0), (1, 2, 2)), far[2:], query_grad, *places)
    query_grad = assembled(((0, 2, 0), (0, 2, 2)), far[:2], query_grad, *places)
    return (query_grad, loss_value.reshape(()))


def solution(mesh):
    finer = Mesh(
        mesh.devices.reshape(mesh.shape["batch"], 4, 4, 8),
        ("batch", X, Y, Z),
    )
    return jax.shard_map(
        local,
        mesh=finer,
        in_specs=(P("batch", None), P(QUEUE, None), P("batch", QUEUE), P("batch")),
        out_specs=(P("batch", None), P()),
        check_vma=False,
    )
```
